128 devices in a mesh: section: 2 (over x_lo), fsdp: 64 (over z, y, x_hi, core).
Axes of the slice: x: 4 (x_hi: 2, x_lo: 2; x = x_hi * 2 + x_lo), y: 4, z: 4, core: 2. Of those that a mesh axis runs over, the one named last changes fastest.
Arguments:
- section_feeds: bfloat16 [2, 2, 4096, 16384], P('section', None, 'fsdp'), may hold values from -6 to 6
- adapter_weights: bfloat16 [2, 16384, 384], P('section', 'fsdp'), as said below
Outputs:
- results: bfloat16 [2, 2, 4096, 16384], P('section', None, 'fsdp')
- weight_grads: bfloat16 [2, 16384, 384], P('section', 'fsdp')
The draws below stay inside these ranges and needn't reach their ends.
Inputs may be any that keep to these rules, and one draw needn't show every extreme that they name: `adapter_weights`: entries of the down projection have spread about 16384^-0.5 and those of the transposed up projection about 192^-0.5.
All inputs are finite; a program needn't handle non-finite values.
Results may differ from the reference program's by a relative error of at most 0.0075.
Values may be sent and summed in bfloat16 or wider, within the bound.
A program may use at most 128 MiB of HBM per device.

```python
import jax
import jax.numpy as jnp
from jax import lax

D = 16384
RANK = 192
MB = 2
TOKENS = 4096
SECTIONS = 2


def draw_adapter_weights(key, part):
    key = jax.random.fold_in(key, 1)
    base = jax.random.normal(key, (SECTIONS, D, 2 * RANK), jnp.float32)
    column = jnp.arange(2 * RANK)
    scale = jnp.where(column < RANK, float(D) ** (-0.5), float(RANK) ** (-0.5))
    return (base * scale).astype(jnp.bfloat16)


def level_of(stream_key, extent, cuts, smallest, largest):
    level = 1.0
    for axis_at, shards_of in cuts:
        heights = jax.random.uniform(jax.random.fold_in(jax.random.fold_in(stream_key, 6), axis_at), (shards_of,), jnp.float32, smallest / len(cuts), largest / len(cuts))
        level = level * jnp.repeat(jnp.exp(heights), extent[axis_at] // shards_of).reshape((-1,) + (1,) * (len(extent) - 1 - axis_at))
    return level


def normal_values(key, extent, deviation, most, shards=(), held_as=jnp.bfloat16):
    entries = jax.random.normal(key, extent, jnp.float32) * deviation
    if len(shards) > 0:
        entries = level_of(key, extent, shards, -0.22, 0.18) * entries
    return jnp.clip(entries, min=-most, max=most).astype(held_as)


def setup_inputs(seed: int = 0) -> dict:
    streams_of = jax.random.split(jax.random.key(seed), 3)
    section_feeds = normal_values(streams_of[0], (SECTIONS, MB, TOKENS, D), 1.0, 6.0, ((0, 2), (2, 64)))
    adapter_weights = draw_adapter_weights(jax.random.fold_in(streams_of[2], 71), 0)
    return dict(section_feeds=section_feeds, adapter_weights=adapter_weights)


EPSILON = 1e-05

def forward(inputs, weight_full):
    low_rank = weight_full.shape[1] // 2
    wide_in = inputs.astype(jnp.float32)
    inverse_rms = lax.rsqrt(lax.optimization_barrier(jnp.mean(wide_in * wide_in, axis=-1, keepdims=True)) + EPSILON)
    normed = (wide_in * inverse_rms).astype(jnp.bfloat16)
    pre_act = jnp.dot(normed, weight_full[:, :low_rank], preferred_element_type=jnp.float32)
    activated = jax.nn.silu(pre_act).astype(jnp.bfloat16)
    branch = lax.dot_general(activated, weight_full[:, low_rank:], (((1,), (1,)), ((), ())), preferred_element_type=jnp.float32)
    return ((wide_in + branch).astype(jnp.bfloat16), normed, pre_act, activated, inverse_rms)

def backward(inputs, upstream, weight_full, pre_act, inverse_rms):
    low_rank = weight_full.shape[1] // 2
    act_grad = jnp.dot(upstream, weight_full[:, low_rank:], preferred_element_type=jnp.float32)
    sigmoid_z = jax.nn.sigmoid(pre_act)
    pre_grad = (act_grad * sigmoid_z * (1.0 + pre_act * (1.0 - sigmoid_z))).astype(jnp.bfloat16)
    norm_grad = lax.dot_general(pre_grad, weight_full[:, :low_rank], (((1,), (1,)), ((), ())), preferred_element_type=jnp.float32)
    wide_in = inputs.astype(jnp.float32)
    cubed = inverse_rms * inverse_rms * inverse_rms
    input_grad = upstream.astype(jnp.float32) + inverse_rms * norm_grad - wide_in * cubed * lax.optimization_barrier(jnp.mean(norm_grad * wide_in, axis=-1, keepdims=True))
    return (input_grad.astype(jnp.bfloat16), pre_grad)

def weight_terms(normed, pre_grad, upstream, activated):
    down_part = lax.dot_general(normed, pre_grad, (((0,), (0,)), ((), ())), preferred_element_type=jnp.float32)
    up_part = lax.dot_general(upstream, activated, (((0,), (0,)), ((), ())), preferred_element_type=jnp.float32)
    return jnp.concatenate([down_part, up_part], axis=1).astype(jnp.bfloat16)

def reference(section_feeds, adapter_weights):
    inputs = section_feeds[0].reshape(MB * TOKENS, D)
    outer_grad = section_feeds[1].reshape(MB * TOKENS, D)
    boundary, normed_a, pre_a, active_a, scale_a = forward(inputs, adapter_weights[0])
    final_out, normed_b, pre_b, active_b, scale_b = forward(boundary, adapter_weights[1])
    passed, grad_b = backward(boundary, outer_grad, adapter_weights[1], pre_b, scale_b)
    input_grad, grad_a = backward(inputs, passed, adapter_weights[0], pre_a, scale_a)
    results = jnp.stack([input_grad, final_out]).reshape(SECTIONS, MB, TOKENS, D)
    grads = jnp.stack([weight_terms(normed_a, grad_a, passed, active_a), weight_terms(normed_b, grad_b, outer_grad, active_b)])
    return (results, grads)
```

```python
import functools

import jax
import jax.numpy as jnp
from jax import lax
from jax.experimental import pallas as pl
from jax.experimental.pallas import tpu as pltpu
from jax.sharding import PartitionSpec as P

MESH = pl.DeviceIdType.MESH
EPSILON = 1e-05
BF = jnp.bfloat16
F32 = jnp.float32
NT = (((1,), (1,)), ((), ()))
NN = (((1,), (0,)), ((), ()))
D = 16384
RANK = 192
ROWS = 128
HALF = D // 2
BLK = 256
UNIT = 2 * BLK
EARLY = 9


def dot(a, b, dims):
    return lax.dot_general(a, b, dims, preferred_element_type=F32)


def dot_wide(a, b, dims):
    high = b.astype(BF)
    low = (b - high.astype(F32)).astype(BF)
    return dot(a, high, dims) + dot(a, low, dims)


def away(i):
    return lax.rem(2 + (i * (i + 1)) // 2, 4)


def kernel(
    feed, wt, res, wg,
    own, oth, w, out, gp, r1, r2, send3, r3,
    part, gram, sq, got_part, got_gram, got_sq, sg, got_sg, lr, bg, lrt,
    own_ss, own_rs, own_ls, ex_ss, ex_rs, pre_ss, pre_rs, pre_ls,
    ag_ss, ag_rs, core_ss, core_rs, sg_ss, sg_rs, lr_ss, lr_rs,
    p1_ss, p1_rs, p2_ss, p2_rs, p3_ss, p3_rs, out_ss, out_rs, out_ls,
):
    s = lax.axis_index("section")
    f = lax.axis_index("fsdp")
    c = lax.rem(f, 2)
    xh = lax.rem(f // 2, 2)
    y = lax.rem(f // 4, 4)
    z = f // 16

    def dev(ss=0, dx=0, dy=0, dz=0, dc=0):
        sx = lax.rem(s + ss, 2)
        at = (lax.rem(z + dz, 4) * 4 + lax.rem(y + dy, 4)) * 2 + lax.rem(xh + dx, 2)
        return (sx, at * 2 + lax.rem(c + dc, 2))

    def remote(src, dst, ssem, rsem, to):
        return pltpu.make_async_remote_copy(
            src_ref=src, dst_ref=dst, send_sem=ssem, recv_sem=rsem,
            device_id=to, device_id_type=MESH)

    peers = [dict(dc=1), dict(ss=1), dict(ss=1, dc=1), dict(dx=1), dict(ss=1, dx=1)]
    peers += [dict(dy=d) for d in (1, 2, 3)] + [dict(dz=d) for d in (1, 2, 3)]
    barrier = pltpu.get_barrier_semaphore()
    for peer in peers:
        pl.semaphore_signal(barrier, inc=1, device_id=dev(**peer), device_id_type=MESH)
    pl.semaphore_wait(barrier, len(peers))

    def lanes(dy, dz, h, width=BLK):
        jj = (lax.rem(z + dz, 4) * 4 + lax.rem(y + dy, 4)) * 2 + h
        return pl.ds(pl.multiple_of(jj * BLK, BLK), width)

    def common_rows(section):
        return pl.ds(pl.multiple_of(section * 2 * RANK, RANK), RANK)

    private_rows = pl.ds(RANK, RANK)
    mine = lanes(0, 0, xh)
    place_c = w.at[common_rows(s), mine]
    place_p = w.at[private_rows, mine]
    pre = [
        remote(wt.at[pl.ds(0, RANK)], place_c, pre_ss.at[0], pre_rs.at[0], dev(ss=1)),
        remote(wt.at[pl.ds(0, RANK)], place_c, pre_ss.at[1], pre_rs.at[1], dev(dx=1)),
        remote(wt.at[pl.ds(RANK, RANK)], place_p, pre_ss.at[2], pre_rs.at[2], dev(dx=1)),
        remote(wt.at[pl.ds(0, RANK)], place_c, pre_ss.at[3], pre_rs.at[3], dev(ss=1, dx=1)),
    ]
    for copy in pre:
        copy.start()
    local_pre = [
        pltpu.make_async_copy(wt.at[pl.ds(0, RANK)], place_c, pre_ls.at[0]),
        pltpu.make_async_copy(wt.at[pl.ds(RANK, RANK)], place_p, pre_ls.at[1]),
    ]
    for copy in local_pre:
        copy.start()

    my_rows = pl.ds(pl.multiple_of(c * ROWS, ROWS), ROWS)
    other_rows = pl.ds(pl.multiple_of((1 - c) * ROWS, ROWS), ROWS)

    def feed_at(jj, core):
        return pl.ds(pl.multiple_of(jj * UNIT + core * BLK, BLK), BLK)

    @pl.loop(0, HALF // BLK)
    def _(jj):
        at = pl.ds(pl.multiple_of(jj * BLK, BLK), BLK)
        remote(feed.at[:, feed_at(jj, 1 - c)], own.at[my_rows, at], own_ss, own_rs, dev(dc=1)).start()
        pltpu.make_async_copy(feed.at[:, feed_at(jj, c)], own.at[my_rows, at], own_ls).start()

    def exchange(i):
        dy, dz = away(i // 4), away(lax.rem(i, 4))
        for h in range(2):
            jj = (lax.rem(z + dz, 4) * 4 + lax.rem(y + dy, 4)) * 2 + h
            at = pl.ds(pl.multiple_of(jj * BLK, BLK), BLK)
            for dc in range(2):
                remote(
                    feed.at[:, feed_at(jj, lax.rem(c + dc, 2))], oth.at[my_rows, at],
                    ex_ss, ex_rs.at[i], dev(ss=1, dc=dc)).start()

    pl.loop(0, EARLY)(exchange)

    halves = (pl.ds(0, 3 * RANK // 2), pl.ds(3 * RANK // 2, 3 * RANK // 2))

    def step(h, oa, ob, along_b):
        pass

    def spot(h, oa, ob, rows=slice(None)):
        at = lanes(oa % 4, ob % 4, h) if h == 0 else lanes(ob % 4, oa % 4, h)
        return w.at[rows, at]

    def near(h, b, d):
        return dev(dy=d % 4) if (h == 0) != b else dev(dz=d % 4)

    started = []

    def go(ref, h, g, k, to):
        copy = remote(ref, ref, ag_ss.at[h, g, k], ag_rs.at[h, g, k], to)
        copy.start()
        started.append(copy)

    def came(ref, h, g, k):
        remote(ref, ref, ag_ss.at[h, g, k], ag_rs.at[h, g, k], dev(dy=1)).wait_recv()

    groups = (0, -1, 1, 2)

    def first_sends(h):
        for k, d in ((0, 1), (1, -1)):
            go(spot(h, 0, 0), h, 0, k, near(h, False, d))
        group_sends(h, 1)

    def group_sends(h, g):
        oa = groups[g - 1]
        for k, d in ((0, 1), (1, -1)):
            go(spot(h, oa, 0), h, g, k, near(h, True, d))

    for copy in local_pre:
        copy.wait()

    def arrived(dxh, section, row, k):
        ref = w.at[row, lanes(0, 0, lax.rem(xh + dxh, 2))]
        remote(ref, ref, pre_ss.at[k], pre_rs.at[k], dev(ss=1)).wait_recv()

    arrived(0, 1 - s, common_rows(1 - s), 0)
    arrived(1, s, common_rows(s), 1)
    arrived(1, s, private_rows, 2)
    arrived(1, 1 - s, common_rows(1 - s), 3)
    for h in range(2):
        first_sends(h)
    for h in range(2):
        came(spot(h, -1, 0), h, 0, 0)
        go(spot(h, -1, 0, halves[0]), h, 0, 2, near(h, False, 1))
        group_sends(h, 2)
        came(spot(h, 1, 0), h, 0, 1)
        go(spot(h, 1, 0, halves[1]), h, 0, 3, near(h, False, -1))
        group_sends(h, 3)

    def forward(h, g):
        oa = groups[g - 1]
        came(spot(h, oa, -1), h, g, 0)
        go(spot(h, oa, -1, halves[0]), h, g, 2, near(h, True, 1))
        came(spot(h, oa, 1), h, g, 1)
        go(spot(h, oa, 1, halves[1]), h, g, 3, near(h, True, -1))

    for h in range(2):
        forward(h, 1)
    for h in range(2):
        came(spot(h, 2, 0, halves[0]), h, 0, 2)
        came(spot(h, 2, 0, halves[1]), h, 0, 3)
        group_sends(h, 4)
    for g in (2, 3, 4):
        for h in range(2):
            forward(h, g)
    for g in (1, 2, 3, 4):
        for h in range(2):
            oa = groups[g - 1]
            came(spot(h, oa, 2, halves[0]), h, g, 2)
            came(spot(h, oa, 2, halves[1]), h, g, 3)

    whole = own.at[my_rows, :]
    pltpu.make_async_copy(whole, whole, own_ls).wait()
    there = own.at[other_rows, :]
    remote(there, there, own_ss, own_rs, dev(dc=1)).wait_recv()
    part[...] = jnp.zeros_like(part)
    gram[...] = jnp.zeros_like(gram)
    sq[...] = jnp.zeros_like(sq)

    @pl.loop(0, HALF // 1024)
    def _(k):
        at = pl.ds(pl.multiple_of(k * 1024, 1024), 1024)
        x = own[:, at]
        for m in range(3):
            part[m] += dot(x, w[pl.ds(m * RANK, RANK), at], NT)
        u = w[pl.ds(0, RANK), at]
        gram[0] += dot(u, u, NT)
        gram[1] += dot(u, w[pl.ds(2 * RANK, RANK), at], NT)
        xf = x.astype(F32)
        sq[...] += jnp.broadcast_to(jnp.sum(xf * xf, axis=1, keepdims=True), sq.shape)

    to_core = [
        remote(part.at[:, other_rows], got_part, core_ss.at[0], core_rs.at[0], dev(dc=1)),
        remote(gram, got_gram, core_ss.at[1], core_rs.at[1], dev(dc=1)),
        remote(sq.at[other_rows], got_sq, core_ss.at[2], core_rs.at[2], dev(dc=1)),
    ]
    for copy in to_core:
        copy.start()
    for copy in to_core:
        copy.wait()
    sums = [part[m, my_rows] + got_part[m] for m in range(3)]
    from_later = remote(sg, got_sg, sg_ss, sg_rs, dev(ss=1))

    lr_mine = lr.at[:, my_rows]
    bg_mine = bg.at[:, my_rows]
    three = lr.at[pl.ds(0, 3), my_rows]
    to_lr = [
        remote(three, three, lr_ss.at[0], lr_rs.at[c], dev(ss=1)),
        remote(three, three, lr_ss.at[1], lr_rs.at[c], dev(ss=1, dc=1)),
        remote(lr_mine, lr_mine, lr_ss.at[2], lr_rs.at[2], dev(dc=1)),
        remote(bg_mine, bg_mine, lr_ss.at[3], lr_rs.at[3], dev(dc=1)),
    ]

    @pl.when(s == 1)
    def _():
        sg[0] = sums[0]
        sg[1] = sums[1]
        from_later.start()
        from_later.wait_send()
        for core in range(2):
            ref = lr.at[pl.ds(0, 3), pl.ds(core * ROWS, ROWS)]
            remote(ref, ref, lr_ss.at[0], lr_rs.at[core], dev(ss=1)).wait_recv()

    @pl.when(s == 0)
    def _():
        from_later.wait_recv()
        q0, p0, r = sums
        g0, g1 = got_sg[0], got_sg[1]
        uu = gram[0] + got_gram[0]
        ua = gram[1] + got_gram[1]
        sx = (sq[my_rows] + got_sq[...])[:, :1]
        inv0 = lax.rsqrt(sx * (1.0 / D) + EPSILON)
        pre0 = p0 * inv0
        sig0 = 1.0 / (1.0 + jnp.exp(-pre0))
        act0 = (pre0 * sig0).astype(BF)
        act0f = act0.astype(F32)
        t = dot_wide(act0, uu, NN)
        sb = sx + jnp.sum(act0f * (2.0 * q0 + t), axis=1, keepdims=True)
        inv1 = lax.rsqrt(jnp.maximum(sb, 0.0) * (1.0 / D) + EPSILON)
        p1 = r + dot_wide(act0, ua, NN)
        pre1 = p1 * inv1
        sig1 = 1.0 / (1.0 + jnp.exp(-pre1))
        act1 = (pre1 * sig1).astype(BF)
        pg1 = (g1 * sig1 * (1.0 + pre1 * (1.0 - sig1))).astype(BF).astype(F32)
        beta = inv1 * inv1 * inv1 * (jnp.sum(pg1 * p1, axis=1, keepdims=True) * (1.0 / D))
        pg1s = (pg1 * inv1).astype(BF)
        ag0 = g0 + dot_wide(pg1s, ua, NT) - beta * (q0 + t)
        pg0 = (ag0 * sig0 * (1.0 + pre0 * (1.0 - sig0))).astype(BF).astype(F32)
        gamma = inv0 * inv0 * inv0 * (jnp.sum(pg0 * p0, axis=1, keepdims=True) * (1.0 / D))
        lr[0, my_rows] = act0
        lr[1, my_rows] = pg1s
        lr[2, my_rows] = act1
        lr[3, my_rows] = (pg0 * inv0).astype(BF)
        bg[0, my_rows] = jnp.broadcast_to(beta, (ROWS, 128))
        bg[1, my_rows] = jnp.broadcast_to(gamma, (ROWS, 128))
        for copy in to_lr:
            copy.start()
        lr_other = lr.at[:, other_rows]
        bg_other = bg.at[:, other_rows]
        remote(lr_other, lr_other, lr_ss.at[2], lr_rs.at[2], dev(dc=1)).wait_recv()
        remote(bg_other, bg_other, lr_ss.at[3], lr_rs.at[3], dev(dc=1)).wait_recv()
        for copy in to_lr:
            copy.wait_send()

    pl.loop(EARLY, 16)(exchange)

    @pl.when(s == 0)
    def _():
        lrt[0] = lr[3].astype(F32).T.astype(BF)
        lrt[1] = lr[0].astype(F32).T.astype(BF)

    @pl.when(s == 1)
    def _():
        lrt[0] = lr[1].astype(F32).T.astype(BF)
        lrt[1] = lr[2].astype(F32).T.astype(BF)

    @pl.loop(0, 16)
    def _(i):
        dy, dz = away(i // 4), away(lax.rem(i, 4))
        jj = (lax.rem(z + dz, 4) * 4 + lax.rem(y + dy, 4)) * 2
        at = pl.ds(pl.multiple_of(jj * BLK, UNIT), UNIT)
        new = oth.at[:, at]
        remote(new, new, ex_ss, ex_rs.at[i], dev(ss=1)).wait_recv()
        u0 = w[pl.ds(0, RANK), at]
        v = w[pl.ds(RANK, RANK), at]
        a1 = w[pl.ds(2 * RANK, RANK), at]

        @pl.when(s == 0)
        def _():
            x, g = own[:, at], oth[:, at]
            xf = x.astype(F32)
            beta = bg[0][:, :1]
            gamma = bg[1][:, :1]
            b = (xf + dot(lr[0], u0, NN)).astype(BF).astype(F32)
            passed = (g.astype(F32) + dot(lr[1], a1, NN) - beta * b).astype(BF)
            out[:, at] = (passed.astype(F32) + dot(lr[3], v, NN) - gamma * xf).astype(BF)
            gp[pl.ds(0, RANK), at] = dot(lrt[0], x, NN).astype(BF)
            gp[pl.ds(RANK, RANK), at] = dot(lrt[1], passed, NN).astype(BF)

        @pl.when(s == 1)
        def _():
            x, g = oth[:, at], own[:, at]
            b = (x.astype(F32) + dot(lr[0], u0, NN)).astype(BF)
            out[:, at] = (b.astype(F32) + dot(lr[2], v, NN)).astype(BF)
            gp[pl.ds(0, RANK), at] = dot(lrt[0], b, NN).astype(BF)
            gp[pl.ds(RANK, RANK), at] = dot(lrt[1], g, NN).astype(BF)

        for h in range(2):
            here = pl.ds(pl.multiple_of((jj + h) * BLK, BLK), BLK)
            there = res.at[:, feed_at(jj + h, c)]
            pltpu.make_async_copy(out.at[my_rows, here], there, out_ls).start()
            remote(out.at[other_rows, here], there, out_ss, out_rs, dev(dc=1)).start()

        @pl.when(dy != 0)
        def _():
            dst = r1.at[0, dy - 1, :, pl.ds(pl.multiple_of(dz * UNIT, UNIT), UNIT)]
            remote(gp.at[pl.ds(0, RANK), at], dst, p1_ss.at[0], p1_rs.at[0, dy - 1, dz], dev(dy=dy)).start()

        @pl.when(dz != 0)
        def _():
            dst = r1.at[1, dz - 1, :, pl.ds(pl.multiple_of(dy * UNIT, UNIT), UNIT)]
            remote(gp.at[pl.ds(RANK, RANK), at], dst, p1_ss.at[1], p1_rs.at[1, dz - 1, dy], dev(dz=dz)).start()

    second = []
    for d in (2, 1, 3, 0):
        for h in (1, 0):
            at = lanes(0, d, 0, UNIT) if h == 0 else lanes(d, 0, 0, UNIT)
            ref = gp.at[pl.ds(h * RANK, RANK), at]
            total = ref[...].astype(F32)
            for k in range(3):
                src = r1.at[h, k, :, pl.ds(d * UNIT, UNIT)]
                remote(src, src, p1_ss.at[h], p1_rs.at[h, k, d], dev(dy=1)).wait_recv()
                total += src[...].astype(F32)
            ref[...] = total.astype(BF)
            if d:
                to = dev(dz=d) if h == 0 else dev(dy=d)
                copy = remote(ref, r2.at[h, d - 1], p2_ss.at[h, d - 1], p2_rs.at[h, d - 1], to)
                copy.start()
                second.append(copy)
    for copy in second:
        copy.wait()
    third = []
    for h in range(2):
        total = gp[pl.ds(h * RANK, RANK), lanes(0, 0, 0, UNIT)].astype(F32)
        for k in range(3):
            total += r2[h, k].astype(F32)
        low = xh == 0
        wg[pl.ds(h * RANK, RANK)] = jnp.where(low, total[:, :BLK], total[:, BLK:])
        send3[h] = jnp.where(low, total[:, BLK:], total[:, :BLK]).astype(BF)
        copy = remote(send3.at[h], r3.at[h], p3_ss.at[h], p3_rs.at[h], dev(dx=1))
        copy.start()
        third.append(copy)
    for h, copy in enumerate(third):
        copy.wait()
        wg[pl.ds(h * RANK, RANK)] += r3[h].astype(F32)

    for copy in pre + started:
        copy.wait_send()
    remote(there_all(own, other_rows), there_all(own, other_rows), own_ss, own_rs, dev(dc=1)).wait_send()
    remote(oth, oth, ex_ss, ex_rs.at[0], dev(ss=1)).wait_send()

    @pl.when(s == 1)
    def _():
        pass

    for h in range(2):
        ref = gp.at[pl.ds(h * RANK, RANK), pl.ds(0, 12 * UNIT)]
        remote(ref, ref, p1_ss.at[h], p1_rs.at[h, 0, 0], dev(dy=1)).wait_send()
    half = out.at[my_rows, :]
    pltpu.make_async_copy(half, half, out_ls).wait()
    remote(half, half, out_ss, out_rs, dev(dc=1)).wait()


def there_all(ref, rows):
    return ref.at[rows, :]


def per_device(section_feeds, adapter_weights):
    shard = adapter_weights[0]
    feed = section_feeds[0].reshape(ROWS, D)
    first = lax.axis_index("section") == 0
    down, up = shard[:, :RANK].T, shard[:, RANK:].T
    wt = jnp.where(first, jnp.concatenate([up, down]), jnp.concatenate([down, up]))
    dma = pltpu.SemaphoreType.DMA
    vm = pltpu.VMEM
    res, wg = pl.pallas_call(
        kernel,
        out_shape=(jax.ShapeDtypeStruct((ROWS, D), BF), jax.ShapeDtypeStruct((2 * RANK, BLK), F32)),
        in_specs=[pl.BlockSpec(memory_space=pl.ANY), pl.BlockSpec(memory_space=pltpu.VMEM)],
        out_specs=(pl.BlockSpec(memory_space=pl.ANY), pl.BlockSpec(memory_space=pltpu.VMEM)),
        scratch_shapes=[
            vm((2 * ROWS, HALF), BF), vm((2 * ROWS, HALF), BF), vm((3 * RANK, HALF), BF),
            vm((2 * ROWS, HALF), BF), vm((2 * RANK, HALF), BF),
            vm((2, 3, RANK, 4 * UNIT), BF), vm((2, 3, RANK, UNIT), BF),
            vm((2, RANK, BLK), BF), vm((2, RANK, BLK), BF),
            vm((3, 2 * ROWS, RANK), F32), vm((2, RANK, RANK), F32), vm((2 * ROWS, 128), F32),
            vm((3, ROWS, RANK), F32), vm((2, RANK, RANK), F32), vm((ROWS, 128), F32),
            vm((2, ROWS, RANK), F32), vm((2, ROWS, RANK), F32),
            vm((4, 2 * ROWS, RANK), BF), vm((2, 2 * ROWS, 128), F32), vm((2, RANK, 2 * ROWS), BF),
            dma, dma, dma, dma, dma((16,)), dma((4,)), dma((4,)), dma((2,)),
            dma((2, 5, 4)), dma((2, 5, 4)), dma((3,)), dma((3,)), dma, dma, dma((4,)), dma((4,)),
            dma((2,)), dma((2, 3, 4)), dma((2, 3)), dma((2, 3)), dma((2,)), dma((2,)), dma, dma, dma,
        ],
        compiler_params=pltpu.CompilerParams(
            collective_id=0, has_side_effects=True, vmem_limit_bytes=60 * 2**20),
        cost_estimate=pl.CostEstimate(flops=8 * 10**9, bytes_accessed=10**7, transcendentals=0),
        name="relay",
    )(feed, wt)
    return res.reshape(section_feeds.shape), wg.T.astype(BF)[None]


def solution(mesh):
    placed = (P("section", None, "fsdp", None), P("section", "fsdp", None))
    return jax.shard_map(per_device, mesh=mesh, in_specs=placed, out_specs=placed, check_vma=False)
```

```python
import jax
import jax.numpy as jnp
from jax import lax
from jax.experimental import pallas as pl
from jax.experimental.pallas import tpu as pltpu
from jax.sharding import PartitionSpec as P

MESH = pl.DeviceIdType.MESH
EPSILON = 1e-05
BF = jnp.bfloat16
F32 = jnp.float32
NT = (((1,), (1,)), ((), ()))
NN = (((1,), (0,)), ((), ()))
D = 16384
RANK = 192
ROWS = 128
HALF = D // 2
BLK = 256
RING = 4 * BLK
PACE = ((2, 4, 5, 6, 7, 9, 10), (2, 3, 4, 5, 6, 6, 6))
FROM_BACK = (2, 3, 1, 0)


def dot(a, b, dims):
    return lax.dot_general(a, b, dims, preferred_element_type=F32)


def dot_wide(a, b, dims):
    high = b.astype(BF)
    low = (b - high.astype(F32)).astype(BF)
    return dot(a, high, dims) + dot(a, low, dims)


def away(i):
    return lax.rem(2 + (i * (i + 1)) // 2, 4)


def kernel(
    feed, wt, res, wg,
    own, oth, w, out, gp, r0, r1, r2, tot, send3, r3,
    part, gram, sq, got_part, got_gram, got_sq, sg, got_sg, lr, bg, lrt,
    own_ss, own_rs, own_ls, ex_ss, ex_rs, pre_ss, pre_rs, pre_ls,
    ag_ss, ag_rs, core_ss, core_rs, sg_ss, sg_rs, lr_ss, lr_rs,
    p0_ss, p0_rs, p1_ss, p1_rs, p2_ss, p2_rs, p3_ss, p3_rs, out_ss, out_rs, out_ls,
):
    s = lax.axis_index("section")
    f = lax.axis_index("fsdp")
    c = lax.rem(f, 2)
    xh = lax.rem(f // 2, 2)
    y = lax.rem(f // 4, 4)
    z = f // 16

    def dev(ss=0, dx=0, dy=0, dz=0, dc=0):
        sx = lax.rem(s + ss, 2)
        at = (lax.rem(z + dz, 4) * 4 + lax.rem(y + dy, 4)) * 2 + lax.rem(xh + dx, 2)
        return (sx, at * 2 + lax.rem(c + dc, 2))

    def remote(src, dst, ssem, rsem, to):
        return pltpu.make_async_remote_copy(
            src_ref=src, dst_ref=dst, send_sem=ssem, recv_sem=rsem,
            device_id=to, device_id_type=MESH)

    other_core, later = dev(dc=1), dev(ss=1)

    def place(r, oa, ob):
        pa, pb = y * (1 - r) + z * r, z * (1 - r) + y * r
        return lax.rem(pa + oa, 4), lax.rem(pb + ob, 4)

    def lanes(r, oa, ob):
        a, b = place(r, oa, ob)
        return pl.ds(pl.multiple_of(((r * 4 + a) * 4 + b) * BLK, BLK), BLK)

    def group_lanes(r, oa):
        a, _ = place(r, oa, 0)
        return pl.ds(pl.multiple_of((r * 4 + a) * RING, RING), RING)

    def feed_at(r, a, b, core):
        jj = (b * (1 - r) + a * r) * 4 + a * (1 - r) + b * r
        return pl.ds(pl.multiple_of(((jj * 2 + lax.rem(xh + r, 2)) * 2 + core) * BLK, BLK), BLK)

    def along(r, d, second):
        if isinstance(r, int):
            return dev(dy=d) if (r == 0) != second else dev(dz=d)
        return dev(dy=d * (1 - r), dz=d * r) if not second else dev(dy=d * r, dz=d * (1 - r))

    peers = [dict(dc=1), dict(ss=1), dict(ss=1, dc=1), dict(dx=1), dict(ss=1, dx=1)]
    peers += [dict(dy=d) for d in (1, 2, 3)] + [dict(dz=d) for d in (1, 2, 3)]
    barrier = pltpu.get_barrier_semaphore()
    for peer in peers:
        pl.semaphore_signal(barrier, inc=1, device_id=dev(**peer), device_id_type=MESH)
    pl.semaphore_wait(barrier, len(peers))

    my_rows = pl.ds(pl.multiple_of(c * ROWS, ROWS), ROWS)
    other_rows = pl.ds(pl.multiple_of((1 - c) * ROWS, ROWS), ROWS)

    def exchange(i):
        for r in range(2):
            oa, ob = away(i // 4), away(lax.rem(i, 4))
            a, b = place(r, oa, ob)
            for dc in range(2):
                remote(
                    feed.at[:, feed_at(r, a, b, lax.rem(c + dc, 2))], oth.at[my_rows, lanes(r, oa, ob)],
                    ex_ss, ex_rs.at[i, r], dev(ss=1, dc=dc)).start()

    def fill():
        @pl.loop(0, 32)
        def _(k):
            r, a, b = k // 16, lax.rem(k // 4, 4), lax.rem(k, 4)
            at = pl.ds(pl.multiple_of(k * BLK, BLK), BLK)
            remote(feed.at[:, feed_at(r, a, b, 1 - c)], own.at[my_rows, at], own_ss, own_rs, other_core).start()
            pltpu.make_async_copy(feed.at[:, feed_at(r, a, b, c)], own.at[my_rows, at], own_ls).start()

    def filled():
        whole = own.at[my_rows, :]
        pltpu.make_async_copy(whole, whole, own_ls).wait()
        there = own.at[other_rows, :]
        remote(there, there, own_ss, own_rs, other_core).wait_recv()

    def gather(section):
        rows = (3 if section == 0 else 2) * RANK
        halves = (pl.ds(0, rows // 2), pl.ds(rows // 2, rows // 2))
        begun = 0
        points = iter(PACE[section])

        def pace():
            nonlocal begun
            upto = next(points)
            if upto > begun:
                pl.loop(begun, upto)(exchange)
            begun = upto

        near, far = lanes(0, 0, 0), lanes(1, 0, 0)
        first, both = pl.ds(0, RANK), pl.ds(0, 2 * RANK)
        middle, last = pl.ds(RANK, RANK), pl.ds(2 * RANK, RANK)
        sent, kept = (first, both) if section == 0 else (last, middle)
        got = last if section == 0 else first
        pre = [
            remote(wt.at[first], w.at[sent, near], pre_ss.at[0], pre_rs.at[0], later),
            remote(wt.at[kept], w.at[kept, far], pre_ss.at[2], pre_rs.at[2], dev(dx=1)),
            remote(wt.at[first], w.at[sent, far], pre_ss.at[1], pre_rs.at[1], dev(ss=1, dx=1)),
        ]
        for copy in pre:
            copy.start()
        local = pltpu.make_async_copy(wt.at[kept], w.at[kept, near], pre_ls)
        local.start()
        pace()

        def arrived(rows, at, k):
            remote(w.at[rows, at], w.at[rows, at], pre_ss.at[k], pre_rs.at[k], later).wait_recv()

        def spot(r, oa, ob, part_rows=pl.ds(0, rows)):
            return w.at[part_rows, lanes(r, oa % 4, ob % 4)]

        started = list(pre)

        def go(ref, r, g, k, to):
            copy = remote(ref, ref, ag_ss.at[r, g, k], ag_rs.at[r, g, k], to)
            copy.start()
            started.append(copy)

        def came(ref, r, g, k):
            remote(ref, ref, ag_ss.at[r, g, k], ag_rs.at[r, g, k], later).wait_recv()

        order = (0, -1, 1, 2)

        def group_sends(r, g):
            for k, d in ((0, 1), (1, 3)):
                go(spot(r, order[g - 1], 0), r, g, k, along(r, d, True))

        def first_sends(r):
            for k, d in ((0, 1), (1, 3)):
                go(spot(r, 0, 0), r, 0, k, along(r, d, False))
            group_sends(r, 1)

        def forward(r, g):
            oa = order[g - 1]
            came(spot(r, oa, -1), r, g, 0)
            go(spot(r, oa, -1, halves[0]), r, g, 2, along(r, 1, True))
            came(spot(r, oa, 1), r, g, 1)
            go(spot(r, oa, 1, halves[1]), r, g, 3, along(r, 3, True))

        def complete(r, g):
            oa = order[g - 1]
            came(spot(r, oa, 2, halves[0]), r, g, 2)
            came(spot(r, oa, 2, halves[1]), r, g, 3)

        def products(g):
            @pl.loop(0, 2)
            def _(r):
                at = group_lanes(r, order[g - 1] % 4)
                x = own[:, at]
                for m in range(3 if section == 0 else 2):
                    part[m] += dot(x, w[pl.ds(m * RANK, RANK), at], NT)
                if section == 0:
                    u = w[pl.ds(0, RANK), at]
                    gram[0] += dot(u, u, NT)
                    gram[1] += dot(u, w[pl.ds(2 * RANK, RANK), at], NT)
                    xf = x.astype(F32)
                    sq[...] += jnp.broadcast_to(jnp.sum(xf * xf, axis=1, keepdims=True), sq.shape)

        local.wait()
        arrived(got, near, 0)
        first_sends(0)
        arrived(kept, far, 2)
        arrived(got, far, 1)
        first_sends(1)
        fill()
        part[...] = jnp.zeros_like(part)
        if section == 0:
            gram[...] = jnp.zeros_like(gram)
            sq[...] = jnp.zeros_like(sq)
        for r in range(2):
            came(spot(r, -1, 0), r, 0, 0)
            go(spot(r, -1, 0, halves[0]), r, 0, 2, along(r, 1, False))
            group_sends(r, 2)
            came(spot(r, 1, 0), r, 0, 1)
            go(spot(r, 1, 0, halves[1]), r, 0, 3, along(r, 3, False))
            group_sends(r, 3)
        pace()
        for r in range(2):
            forward(r, 1)
        for r in range(2):
            came(spot(r, 2, 0, halves[0]), r, 0, 2)
            came(spot(r, 2, 0, halves[1]), r, 0, 3)
            group_sends(r, 4)
        pace()
        filled()
        for g in (2, 3, 4):
            for r in range(2):
                forward(r, g)
            pace()
            for r in range(2):
                complete(r, g - 1)
            products(g - 1)
        for r in range(2):
            complete(r, 4)
        pace()
        products(4)

        to_core = [remote(part.at[:, other_rows], got_part, core_ss.at[0], core_rs.at[0], other_core)]
        if section == 0:
            to_core.append(remote(gram, got_gram, core_ss.at[1], core_rs.at[1], other_core))
            to_core.append(remote(sq.at[other_rows], got_sq, core_ss.at[2], core_rs.at[2], other_core))
        for copy in to_core:
            copy.start()
        for copy in to_core:
            copy.wait()
        for copy in started:
            copy.wait_send()
        return begun

    lr_mine, lr_other = lr.at[:, my_rows], lr.at[:, other_rows]
    bg_mine, bg_other = bg.at[:, my_rows], bg.at[:, other_rows]
    three = lr.at[pl.ds(0, 3), my_rows]
    three_other = lr.at[pl.ds(0, 3), other_rows]
    from_later = remote(sg, got_sg, sg_ss, sg_rs, later)

    @pl.when(s == 1)
    def _():
        begun = gather(1)
        sg[...] = part[pl.ds(0, 2), my_rows] + got_part[pl.ds(0, 2)]
        from_later.start()
        pl.loop(begun, 16)(exchange)
        from_later.wait_send()
        remote(three, three, lr_ss.at[0], lr_rs.at[0], later).wait_recv()
        hand_on = remote(three, three, lr_ss.at[1], lr_rs.at[1], other_core)
        hand_on.start()
        remote(three_other, three_other, lr_ss.at[1], lr_rs.at[1], other_core).wait_recv()
        hand_on.wait_send()
        lrt[0] = lr[1].astype(F32).T.astype(BF)
        lrt[1] = lr[2].astype(F32).T.astype(BF)

    @pl.when(s == 0)
    def _():
        begun = gather(0)
        q0, p0, r = [part[m, my_rows] + got_part[m] for m in range(3)]
        uu = gram[0] + got_gram[0]
        ua = gram[1] + got_gram[1]
        sx = (sq[my_rows] + got_sq[...])[:, :1]
        inv0 = lax.rsqrt(sx * (1.0 / D) + EPSILON)
        pre0 = p0 * inv0
        sig0 = 1.0 / (1.0 + jnp.exp(-pre0))
        act0 = (pre0 * sig0).astype(BF)
        act0f = act0.astype(F32)
        t = dot_wide(act0, uu, NN)
        sb = sx + jnp.sum(act0f * (2.0 * q0 + t), axis=1, keepdims=True)
        inv1 = lax.rsqrt(jnp.maximum(sb, 0.0) * (1.0 / D) + EPSILON)
        p1 = r + dot_wide(act0, ua, NN)
        pre1 = p1 * inv1
        sig1 = 1.0 / (1.0 + jnp.exp(-pre1))
        act1 = (pre1 * sig1).astype(BF)
        from_later.wait_recv()
        g0, g1 = got_sg[0], got_sg[1]
        pg1 = (g1 * sig1 * (1.0 + pre1 * (1.0 - sig1))).astype(BF).astype(F32)
        pg1s = (pg1 * inv1).astype(BF)
        lr[0, my_rows] = act0
        lr[1, my_rows] = pg1s
        lr[2, my_rows] = act1
        to_later = remote(three, three, lr_ss.at[0], lr_rs.at[0], later)
        to_later.start()
        pl.loop(begun, 16)(exchange)
        beta = inv1 * inv1 * inv1 * (jnp.sum(pg1 * p1, axis=1, keepdims=True) * (1.0 / D))
        ag0 = g0 + dot_wide(pg1s, ua, NT) - beta * (q0 + t)
        pg0 = (ag0 * sig0 * (1.0 + pre0 * (1.0 - sig0))).astype(BF).astype(F32)
        gamma = inv0 * inv0 * inv0 * (jnp.sum(pg0 * p0, axis=1, keepdims=True) * (1.0 / D))
        lr[3, my_rows] = (pg0 * inv0).astype(BF)
        bg[0, my_rows] = jnp.broadcast_to(beta, (ROWS, 128))
        bg[1, my_rows] = jnp.broadcast_to(gamma, (ROWS, 128))
        to_other = [
            remote(lr_mine, lr_mine, lr_ss.at[2], lr_rs.at[2], other_core),
            remote(bg_mine, bg_mine, lr_ss.at[3], lr_rs.at[3], other_core),
        ]
        for copy in to_other:
            copy.start()
        remote(lr_other, lr_other, lr_ss.at[2], lr_rs.at[2], other_core).wait_recv()
        remote(bg_other, bg_other, lr_ss.at[3], lr_rs.at[3], other_core).wait_recv()
        for copy in to_other:
            copy.wait_send()
        lrt[0] = lr[3].astype(F32).T.astype(BF)
        lrt[1] = lr[0].astype(F32).T.astype(BF)
        to_later.wait_send()

    top, bottom = pl.ds(0, RANK), pl.ds(RANK, RANK)

    def blocks(n):
        oa = FROM_BACK[n]

        @pl.loop(0, 8)
        def _(j):
            ob, r = away(j // 2), lax.rem(j, 2)
            at = lanes(r, oa, ob)
            a, b = place(r, oa, ob)
            here = pl.ds(pl.multiple_of(ob * BLK, BLK), BLK)
            new = oth.at[:, at]
            remote(new, new, ex_ss, ex_rs.at[n * 4 + j // 2, r], later).wait_recv()
            if oa in (1, 3):
                k, rows = (0, top) if oa == 1 else (1, bottom)
                src = r0.at[r, k, :, here]
                remote(src, src, p0_ss, p0_rs.at[r, k, ob], later).wait_recv()

            def store(down, up):
                if oa == 1:
                    down += r0[r, 0, :, here].astype(F32)
                if oa == 3:
                    up += r0[r, 1, :, here].astype(F32)
                gp[top, at] = down.astype(BF)
                gp[bottom, at] = up.astype(BF)

            @pl.when(s == 0)
            def _():
                x, g = own[:, at], oth[:, at]
                xf = x.astype(F32)
                beta = bg[0][:, :1]
                gamma = bg[1][:, :1]
                bound = (xf + dot(lr[0], w[pl.ds(0, RANK), at], NN)).astype(BF).astype(F32)
                passed = (g.astype(F32) + dot(lr[1], w[pl.ds(2 * RANK, RANK), at], NN) - beta * bound).astype(BF)
                out[:, at] = (passed.astype(F32) + dot(lr[3], w[pl.ds(RANK, RANK), at], NN) - gamma * xf).astype(BF)
                store(dot(lrt[0], x, NN), dot(lrt[1], passed, NN))

            @pl.when(s == 1)
            def _():
                x, g = oth[:, at], own[:, at]
                bound = (x.astype(F32) + dot(lr[0], w[pl.ds(0, RANK), at], NN)).astype(BF)
                out[:, at] = (bound.astype(F32) + dot(lr[2], w[pl.ds(RANK, RANK), at], NN)).astype(BF)
                store(dot(lrt[0], bound, NN), dot(lrt[1], g, NN))

            if oa == 2:
                for k, rows, d in ((0, top, 1), (1, bottom, 3)):
                    remote(gp.at[rows, at], r0.at[r, k, :, here], p0_ss, p0_rs.at[r, k, ob], along(r, d, False)).start()
            elif oa:
                k = 0 if oa == 1 else 1
                remote(gp.at[:, at], r1.at[r, k, :, here], p1_ss, p1_rs.at[r, k, ob], along(r, oa, False)).start()
            there = res.at[:, feed_at(r, a, b, c)]
            pltpu.make_async_copy(out.at[my_rows, at], there, out_ls).start()
            remote(out.at[other_rows, at], there, out_ss, out_rs, other_core).start()
            if oa == 0:
                total = gp[:, at].astype(F32)
                for k in range(2):
                    src = r1.at[r, k, :, here]
                    remote(src, src, p1_ss, p1_rs.at[r, k, ob], later).wait_recv()
                    total += src[...].astype(F32)

                @pl.when(ob == 0)
                def _():
                    tot[r] = total

                @pl.when(ob != 0)
                def _():
                    gp[:, at] = total.astype(BF)
                    remote(gp.at[:, at], r2.at[r, ob - 1], p2_ss, p2_rs.at[r, ob - 1], along(r, ob, True)).start()

    for n in range(4):
        blocks(n)

    def summed(r):
        total = tot[r]
        for k in range(3):
            remote(r2.at[r, k], r2.at[r, k], p2_ss, p2_rs.at[r, k], later).wait_recv()
            total += r2[r, k].astype(F32)
        return total

    send3[...] = summed(1).astype(BF)
    across = remote(send3, r3, p3_ss, p3_rs, dev(dx=1))
    across.start()
    total = summed(0)
    across.wait()
    wg[...] = total + r3[...].astype(F32)

    there = own.at[other_rows, :]
    remote(there, there, own_ss, own_rs, other_core).wait_send()
    remote(oth, oth, ex_ss, ex_rs.at[0, 0], later).wait_send()
    ref = gp.at[top, pl.ds(0, 16 * BLK)]
    remote(ref, ref, p0_ss, p0_rs.at[0, 0, 0], later).wait_send()
    ref = gp.at[:, pl.ds(0, 16 * BLK)]
    remote(ref, ref, p1_ss, p1_rs.at[0, 0, 0], later).wait_send()
    ref = gp.at[:, pl.ds(0, 6 * BLK)]
    remote(ref, ref, p2_ss, p2_rs.at[0, 0], later).wait_send()
    half = out.at[my_rows, :]
    pltpu.make_async_copy(half, half, out_ls).wait()
    remote(half, half, out_ss, out_rs, other_core).wait()


def per_device(section_feeds, adapter_weights):
    shard = adapter_weights[0]
    feed = section_feeds[0].reshape(ROWS, D)
    first = lax.axis_index("section") == 0
    down, up = shard[:, :RANK].T, shard[:, RANK:].T
    wt = jnp.where(first, jnp.concatenate([up, down]), jnp.concatenate([down, up]))
    dma = pltpu.SemaphoreType.DMA
    vm = pltpu.VMEM
    res, wg = pl.pallas_call(
        kernel,
        out_shape=(jax.ShapeDtypeStruct((ROWS, D), BF), jax.ShapeDtypeStruct((2 * RANK, BLK), F32)),
        in_specs=[pl.BlockSpec(memory_space=pl.ANY), pl.BlockSpec(memory_space=pltpu.VMEM)],
        out_specs=(pl.BlockSpec(memory_space=pl.ANY), pl.BlockSpec(memory_space=pltpu.VMEM)),
        scratch_shapes=[
            vm((2 * ROWS, HALF), BF), vm((2 * ROWS, HALF), BF), vm((3 * RANK, HALF), BF),
            vm((2 * ROWS, HALF), BF), vm((2 * RANK, HALF), BF),
            vm((2, 2, RANK, RING), BF), vm((2, 2, 2 * RANK, RING), BF), vm((2, 3, 2 * RANK, BLK), BF),
            vm((2, 2 * RANK, BLK), F32), vm((2 * RANK, BLK), BF), vm((2 * RANK, BLK), BF),
            vm((3, 2 * ROWS, RANK), F32), vm((2, RANK, RANK), F32), vm((2 * ROWS, 128), F32),
            vm((3, ROWS, RANK), F32), vm((2, RANK, RANK), F32), vm((ROWS, 128), F32),
            vm((2, ROWS, RANK), F32), vm((2, ROWS, RANK), F32),
            vm((4, 2 * ROWS, RANK), BF), vm((2, 2 * ROWS, 128), F32), vm((2, RANK, 2 * ROWS), BF),
            dma, dma, dma, dma, dma((16, 2)), dma((3,)), dma((3,)), dma,
            dma((2, 5, 4)), dma((2, 5, 4)), dma((3,)), dma((3,)), dma, dma, dma((4,)), dma((4,)),
            dma, dma((2, 2, 4)), dma, dma((2, 2, 4)), dma, dma((2, 3)), dma, dma, dma, dma, dma,
        ],
        compiler_params=pltpu.CompilerParams(
            collective_id=0, has_side_effects=True, vmem_limit_bytes=60 * 2**20),
        cost_estimate=pl.CostEstimate(flops=8 * 10**9, bytes_accessed=10**7, transcendentals=0),
        name="relay",
    )(feed, wt)
    return res.reshape(section_feeds.shape), wg.T.astype(BF)[None]


def solution(mesh):
    placed = (P("section", None, "fsdp", None), P("section", "fsdp", None))
    return jax.shard_map(per_device, mesh=mesh, in_specs=placed, out_specs=placed, check_vma=False)
```

```python
import jax
import jax.numpy as jnp
from jax import lax
from jax.experimental import pallas as pl
from jax.experimental.pallas import tpu as pltpu
from jax.sharding import PartitionSpec as P

MESH = pl.DeviceIdType.MESH
EPSILON = 1e-05
BF = jnp.bfloat16
F32 = jnp.float32
NT = (((1,), (1,)), ((), ()))
NN = (((1,), (0,)), ((), ()))
D = 16384
RANK = 192
ROWS = 128
HALF = D // 2
BLK = 256
RING = 4 * BLK
PACE = ((2, 4, 5, 6, 7, 8, 9), (3, 5, 6, 7, 8, 9, 9))
FROM_BACK = (2, 3, 1, 0)


def dot(a, b, dims):
    return lax.dot_general(a, b, dims, preferred_element_type=F32)


def dot_wide(a, b, dims):
    high = b.astype(BF)
    low = (b - high.astype(F32)).astype(BF)
    return dot(a, high, dims) + dot(a, low, dims)


def away(i):
    return lax.rem(2 + (i * (i + 1)) // 2, 4)


def kernel(
    feed, shard, res, wg,
    own, oth, w, out, gp, r0, r1, r2, tot, send3, r3,
    part, gram, sq, got_part, got_gram, got_sq, sg, got_sg, lr, bg, lrt,
    own_ss, own_rs, own_ls, ex_ss, ex_rs, pre_ss, pre_rs,
    ag_ss, ag_rs, own_part_ss, ship_ss, ship_rs, core_ss, core_rs, sg_ss, sg_rs, lr_ss, lr_rs,
    p0_ss, p0_rs, p1_ss, p1_rs, p2_ss, p2_rs, p3_ss, p3_rs, out_ss, out_rs, out_ls,
):
    s = lax.axis_index("section")
    f = lax.axis_index("fsdp")
    c = lax.rem(f, 2)
    xh = lax.rem(f // 2, 2)
    y = lax.rem(f // 4, 4)
    z = f // 16

    def dev(ss=0, dx=0, dy=0, dz=0, dc=0):
        sx = lax.rem(s + ss, 2)
        at = (lax.rem(z + dz, 4) * 4 + lax.rem(y + dy, 4)) * 2 + lax.rem(xh + dx, 2)
        return (sx, at * 2 + lax.rem(c + dc, 2))

    def remote(src, dst, ssem, rsem, to):
        return pltpu.make_async_remote_copy(
            src_ref=src, dst_ref=dst, send_sem=ssem, recv_sem=rsem,
            device_id=to, device_id_type=MESH)

    other_core, later = dev(dc=1), dev(ss=1)

    def turned(r, core):
        return lax.rem(r + core, 2)

    def place(r, oa, ob, core=c):
        q = turned(r, core)
        pa, pb = y * (1 - q) + z * q, z * (1 - q) + y * q
        return lax.rem(pa + oa, 4), lax.rem(pb + ob, 4)

    def block(r, a, b):
        return pl.ds(pl.multiple_of(((r * 4 + a) * 4 + b) * BLK, BLK), BLK)

    def lanes(r, oa, ob):
        return block(r, *place(r, oa, ob))

    def group_lanes(r, oa):
        a, _ = place(r, oa, 0)
        return pl.ds(pl.multiple_of((r * 4 + a) * RING, RING), RING)

    def feed_at(r, a, b, core):
        q = turned(r, core)
        jj = (b * (1 - q) + a * q) * 4 + a * (1 - q) + b * q
        return pl.ds(pl.multiple_of(((jj * 2 + lax.rem(xh + r, 2)) * 2 + core) * BLK, BLK), BLK)

    def along(r, d, second):
        q = turned(r + int(second), c)
        return dev(dy=d * (1 - q), dz=d * q)

    peers = [dict(dc=1), dict(ss=1), dict(ss=1, dc=1), dict(dx=1), dict(ss=1, dx=1)]
    peers += [dict(dy=d) for d in (1, 2, 3)] + [dict(dz=d) for d in (1, 2, 3)]
    barrier = pltpu.get_barrier_semaphore()
    for peer in peers:
        pl.semaphore_signal(barrier, inc=1, device_id=dev(**peer), device_id_type=MESH)
    turned_shard = shard[...].astype(F32).T.astype(BF)

    @pl.when(s == 0)
    def _():
        w[pl.ds(0, RANK), lanes(0, 0, 0)] = turned_shard[RANK:]
        w[pl.ds(RANK, RANK), lanes(0, 0, 0)] = turned_shard[:RANK]

    @pl.when(s == 1)
    def _():
        w[pl.ds(2 * RANK, RANK), lanes(0, 0, 0)] = turned_shard[:RANK]
        w[pl.ds(RANK, RANK), lanes(0, 0, 0)] = turned_shard[RANK:]

    pl.semaphore_wait(barrier, len(peers))

    my_rows = pl.ds(pl.multiple_of(c * ROWS, ROWS), ROWS)
    other_rows = pl.ds(pl.multiple_of((1 - c) * ROWS, ROWS), ROWS)

    def exchange(i):
        for r in range(2):
            oa, ob = away(i // 4), away(lax.rem(i, 4))
            for dc in range(2):
                core = lax.rem(c + dc, 2)
                a, b = place(r, oa, ob, core)
                remote(
                    feed.at[:, feed_at(r, a, b, core)], oth.at[my_rows, block(r, a, b)],
                    ex_ss, ex_rs.at[i, r], dev(ss=1, dc=dc)).start()

    def fill():
        @pl.loop(0, 32)
        def _(k):
            r, a, b = k // 16, lax.rem(k // 4, 4), lax.rem(k, 4)
            at = pl.ds(pl.multiple_of(k * BLK, BLK), BLK)
            remote(feed.at[:, feed_at(r, a, b, 1 - c)], own.at[my_rows, at], own_ss, own_rs, other_core).start()
            pltpu.make_async_copy(feed.at[:, feed_at(r, a, b, c)], own.at[my_rows, at], own_ls).start()

    def filled():
        whole = own.at[my_rows, :]
        pltpu.make_async_copy(whole, whole, own_ls).wait()
        there = own.at[other_rows, :]
        remote(there, there, own_ss, own_rs, other_core).wait_recv()

    def gather(section):
        rows = (3 * RANK, 2 * RANK)
        halves = [(pl.ds(0, n // 2), pl.ds(n // 2, n // 2)) for n in rows]
        begun = 0
        points = iter(PACE[section])

        def pace():
            nonlocal begun
            upto = next(points)
            if upto > begun:
                pl.loop(begun, upto)(exchange)
            begun = upto

        near, far = lanes(0, 0, 0), lanes(1, 0, 0)
        first, both = pl.ds(0, RANK), pl.ds(0, 2 * RANK)
        middle, last = pl.ds(RANK, RANK), pl.ds(2 * RANK, RANK)
        sent, kept = (first, both) if section == 0 else (last, middle)
        got = last if section == 0 else first
        diagonal = dev(ss=1, dx=1)
        pre = [
            remote(w.at[sent, near], w.at[sent, near], pre_ss.at[0], pre_rs.at[0], later),
            remote(w.at[kept, near], w.at[kept, far], pre_ss.at[2], pre_rs.at[2], dev(dx=1)),
        ]
        if section == 0:
            pre.append(remote(w.at[first, near], w.at[first, far], pre_ss.at[1], pre_rs.at[1], diagonal))
        for copy in pre:
            copy.start()

        def arrived(rows, at, k):
            remote(w.at[rows, at], w.at[rows, at], pre_ss.at[k], pre_rs.at[k], later).wait_recv()

        def spot(r, oa, ob, part_rows=None):
            return w.at[pl.ds(0, rows[r]) if part_rows is None else part_rows, lanes(r, oa % 4, ob % 4)]

        started = list(pre)

        def go(ref, r, g, k, to, sem=None):
            copy = remote(ref, ref, ag_ss.at[r, g, k] if sem is None else sem, ag_rs.at[r, g, k], to)
            copy.start()
            started.append(copy)

        def came(ref, r, g, k):
            remote(ref, ref, ag_ss.at[r, g, k], ag_rs.at[r, g, k], later).wait_recv()

        order = (0, -1, 1, 2)

        def ship(oa, ob, half=None):
            if section == 0:
                return
            a, b = place(0, oa % 4, ob % 4)
            copy = remote(
                w.at[last, block(0, a, b)], w.at[last, block(1, b, a)], ship_ss.at[a * 4 + b], ship_rs.at[b * 4 + a],
                diagonal)
            copy.start()
            started.append(copy)

        def group_sends(r, g):
            for k, d in ((0, 1), (1, 3)):
                go(spot(r, order[g - 1], 0), r, g, k, along(r, d, True))

        def first_sends(r):
            for k, d in ((0, 1), (1, 3)):
                go(spot(r, 0, 0), r, 0, k, along(r, d, False))
            group_sends(r, 1)

        def forward(r, g):
            oa = order[g - 1]
            for k, d in ((0, -1), (1, 1)):
                came(spot(r, oa, d), r, g, k)
                go(spot(r, oa, d, halves[r][k]), r, g, 2 + k, along(r, -d % 4, True))
                if r == 0:
                    ship(oa, d)

        def complete(r, g):
            oa = order[g - 1]
            came(spot(r, oa, 2, halves[r][0]), r, g, 2)
            came(spot(r, oa, 2, halves[r][1]), r, g, 3)
            if r == 0:
                ship(oa, 2)

        def products(g):
            for r in range(2):
                at = group_lanes(r, order[g - 1] % 4)
                x = own[:, at]
                wide = section == 0 and r == 0
                for m in range(3 if wide else 2):
                    part[m] += dot(x, w[pl.ds(m * RANK, RANK), at], NT)
                if section == 0:
                    u = w[pl.ds(0, RANK), at]
                    gram[0] += dot(u, u, NT)
                    if wide:
                        gram[1] += dot(u, w[last, at], NT)
                    xf = x.astype(F32)
                    sq[...] += jnp.broadcast_to(jnp.sum(xf * xf, axis=1, keepdims=True), sq.shape)

        def far_products():
            for k in range(16):
                ref = w.at[last, pl.ds((16 + k) * BLK, BLK)]
                remote(ref, ref, ship_ss.at[0], ship_rs.at[k], diagonal).wait_recv()

            @pl.loop(0, 4)
            def _(k):
                at = pl.ds(pl.multiple_of((4 + k) * RING, RING), RING)
                part[2] += dot(own[:, at], w[last, at], NT)
                gram[1] += dot(w[pl.ds(0, RANK), at], w[last, at], NT)

        local = both if section == 0 else pl.ds(RANK, 2 * RANK)
        for rows_now, sem in ((local, own_part_ss), (got, None)):
            if sem is None:
                ship(0, 0)
                pace()
                arrived(got, near, 0)
            for second in (False, True):
                for k, d in ((0, 1), (1, 3)):
                    go(spot(0, 0, 0, rows_now), 0, int(second), k, along(0, d, second),
                       None if sem is None else sem.at[int(second), k])
        arrived(kept, far, 2)
        if section == 1:
            arrived(got, far, 1)
        first_sends(1)
        fill()
        part[...] = jnp.zeros_like(part)
        if section == 0:
            gram[...] = jnp.zeros_like(gram)
            sq[...] = jnp.zeros_like(sq)
        for r in range(2):
            for k, d in ((0, -1), (1, 1)):
                came(spot(r, d, 0), r, 0, k)
                go(spot(r, d, 0, halves[r][k]), r, 0, 2 + k, along(r, -d % 4, False))
                group_sends(r, 2 + k)
                if r == 0:
                    ship(d, 0)
        pace()
        for r in range(2):
            forward(r, 1)
        for r in range(2):
            came(spot(r, 2, 0, halves[r][0]), r, 0, 2)
            came(spot(r, 2, 0, halves[r][1]), r, 0, 3)
            group_sends(r, 4)
            if r == 0:
                ship(2, 0)
        pace()
        filled()
        for g in (2, 3, 4):
            for r in range(2):
                forward(r, g)
            pace()
            if g == 3:
                for r in range(2):
                    complete(r, 1)
                products(1)
        for g in (2, 3):
            for r in range(2):
                complete(r, g)
            products(g)
        for r in range(2):
            complete(r, 4)
        pace()
        products(4)

        def to_core(src, dst, k):
            copy = remote(src, dst, core_ss.at[k], core_rs.at[k], other_core)
            copy.start()
            return copy

        two, third = pl.ds(0, 2), pl.ds(2, 1)
        handed = [to_core(part.at[two, other_rows], got_part.at[two], 0)]
        if section == 0:
            handed.append(to_core(gram.at[0], got_gram.at[0], 1))
            handed.append(to_core(sq.at[other_rows], got_sq, 2))
            far_products()
            handed.append(to_core(part.at[third, other_rows], got_part.at[third], 3))
            handed.append(to_core(gram.at[1], got_gram.at[1], 4))
        for copy in handed:
            copy.wait()
        return begun, started

    lr_mine, lr_other = lr.at[:, my_rows], lr.at[:, other_rows]
    bg_mine, bg_other = bg.at[:, my_rows], bg.at[:, other_rows]
    three = lr.at[pl.ds(0, 3), my_rows]
    three_other = lr.at[pl.ds(0, 3), other_rows]
    from_later = remote(sg, got_sg, sg_ss, sg_rs, later)

    @pl.when(s == 1)
    def _():
        begun, started = gather(1)
        sg[...] = part[pl.ds(0, 2), my_rows] + got_part[pl.ds(0, 2)]
        from_later.start()
        pl.loop(begun, 16)(exchange)
        from_later.wait_send()
        remote(three, three, lr_ss.at[0], lr_rs.at[0], later).wait_recv()
        hand_on = remote(three, three, lr_ss.at[1], lr_rs.at[1], other_core)
        hand_on.start()
        remote(three_other, three_other, lr_ss.at[1], lr_rs.at[1], other_core).wait_recv()
        hand_on.wait_send()
        for copy in started:
            copy.wait_send()
        lrt[0] = lr[1].astype(F32).T.astype(BF)
        lrt[1] = lr[2].astype(F32).T.astype(BF)

    @pl.when(s == 0)
    def _():
        begun, started = gather(0)
        q0, p0, r = [part[m, my_rows] + got_part[m] for m in range(3)]
        uu = gram[0] + got_gram[0]
        ua = gram[1] + got_gram[1]
        sx = (sq[my_rows] + got_sq[...])[:, :1]
        inv0 = lax.rsqrt(sx * (1.0 / D) + EPSILON)
        pre0 = p0 * inv0
        sig0 = 1.0 / (1.0 + jnp.exp(-pre0))
        act0 = (pre0 * sig0).astype(BF)
        act0f = act0.astype(F32)
        t = dot_wide(act0, uu, NN)
        sb = sx + jnp.sum(act0f * (2.0 * q0 + t), axis=1, keepdims=True)
        inv1 = lax.rsqrt(jnp.maximum(sb, 0.0) * (1.0 / D) + EPSILON)
        p1 = r + dot_wide(act0, ua, NN)
        pre1 = p1 * inv1
        sig1 = 1.0 / (1.0 + jnp.exp(-pre1))
        act1 = (pre1 * sig1).astype(BF)
        from_later.wait_recv()
        g0, g1 = got_sg[0], got_sg[1]
        pg1 = (g1 * sig1 * (1.0 + pre1 * (1.0 - sig1))).astype(BF).astype(F32)
        pg1s = (pg1 * inv1).astype(BF)
        lr[0, my_rows] = act0
        lr[1, my_rows] = pg1s
        lr[2, my_rows] = act1
        to_later = remote(three, three, lr_ss.at[0], lr_rs.at[0], later)
        to_later.start()
        pl.loop(begun, 16)(exchange)
        beta = inv1 * inv1 * inv1 * (jnp.sum(pg1 * p1, axis=1, keepdims=True) * (1.0 / D))
        ag0 = g0 + dot_wide(pg1s, ua, NT) - beta * (q0 + t)
        pg0 = (ag0 * sig0 * (1.0 + pre0 * (1.0 - sig0))).astype(BF).astype(F32)
        gamma = inv0 * inv0 * inv0 * (jnp.sum(pg0 * p0, axis=1, keepdims=True) * (1.0 / D))
        lr[3, my_rows] = (pg0 * inv0).astype(BF)
        bg[0, my_rows] = jnp.broadcast_to(beta, (ROWS, 128))
        bg[1, my_rows] = jnp.broadcast_to(gamma, (ROWS, 128))
        to_other = [
            remote(lr_mine, lr_mine, lr_ss.at[2], lr_rs.at[2], other_core),
            remote(bg_mine, bg_mine, lr_ss.at[3], lr_rs.at[3], other_core),
        ]
        for copy in to_other:
            copy.start()
        remote(lr_other, lr_other, lr_ss.at[2], lr_rs.at[2], other_core).wait_recv()
        remote(bg_other, bg_other, lr_ss.at[3], lr_rs.at[3], other_core).wait_recv()
        for copy in to_other + started:
            copy.wait_send()
        lrt[0] = lr[3].astype(F32).T.astype(BF)
        lrt[1] = lr[0].astype(F32).T.astype(BF)
        to_later.wait_send()

    top, bottom = pl.ds(0, RANK), pl.ds(RANK, RANK)

    def blocks(n):
        oa = FROM_BACK[n]

        @pl.loop(0, 4)
        def _(j):
            ob = away(j)
            here = pl.ds(pl.multiple_of(ob * BLK, BLK), BLK)
            both = range(2)
            at = [lanes(r, oa, ob) for r in both]
            for r in both:
                new = oth.at[:, at[r]]
                remote(new, new, ex_ss, ex_rs.at[n * 4 + j, r], later).wait_recv()
                if oa in (1, 3):
                    k = oa // 2
                    src = r0.at[r, k, :, here]
                    remote(src, src, p0_ss, p0_rs.at[r, k, ob], later).wait_recv()

            def store(done, down, up):
                if oa == 1:
                    down = [down[r] + r0[r, 0, :, here].astype(F32) for r in both]
                if oa == 3:
                    up = [up[r] + r0[r, 1, :, here].astype(F32) for r in both]
                for r in both:
                    out[:, at[r]] = done[r]
                    gp[top, at[r]] = down[r].astype(BF)
                    gp[bottom, at[r]] = up[r].astype(BF)

            @pl.when(s == 0)
            def _():
                x, g = [own[:, at[r]] for r in both], [oth[:, at[r]] for r in both]
                xf = [x[r].astype(F32) for r in both]
                beta = bg[0][:, :1]
                gamma = bg[1][:, :1]
                grown = [dot(lr[0], w[pl.ds(0, RANK), at[r]], NN) for r in both]
                slope = [dot(lr[1], w[pl.ds(2 * RANK, RANK), at[r]], NN) for r in both]
                bound = [(xf[r] + grown[r]).astype(BF).astype(F32) for r in both]
                passed = [(g[r].astype(F32) + slope[r] - beta * bound[r]).astype(BF) for r in both]
                first = [dot(lr[3], w[pl.ds(RANK, RANK), at[r]], NN) for r in both]
                down = [dot(lrt[0], x[r], NN) for r in both]
                up = [dot(lrt[1], passed[r], NN) for r in both]
                done = [(passed[r].astype(F32) + first[r] - gamma * xf[r]).astype(BF) for r in both]
                store(done, down, up)

            @pl.when(s == 1)
            def _():
                x, g = [oth[:, at[r]] for r in both], [own[:, at[r]] for r in both]
                grown = [dot(lr[0], w[pl.ds(0, RANK), at[r]], NN) for r in both]
                final = [dot(lr[2], w[pl.ds(RANK, RANK), at[r]], NN) for r in both]
                up = [dot(lrt[1], g[r], NN) for r in both]
                bound = [(x[r].astype(F32) + grown[r]).astype(BF) for r in both]
                down = [dot(lrt[0], bound[r], NN) for r in both]
                done = [(bound[r].astype(F32) + final[r]).astype(BF) for r in both]
                store(done, down, up)

            for r in both:
                if oa == 2:
                    for k, rows, d in ((0, top, 1), (1, bottom, 3)):
                        remote(
                            gp.at[rows, at[r]], r0.at[r, k, :, here], p0_ss, p0_rs.at[r, k, ob],
                            along(r, d, False)).start()
                elif oa:
                    k = oa // 2
                    remote(
                        gp.at[:, at[r]], r1.at[r, k, :, here], p1_ss, p1_rs.at[r, k, ob], along(r, oa, False)).start()
            for r in both:
                there = res.at[:, feed_at(r, *place(r, oa, ob), c)]
                pltpu.make_async_copy(out.at[my_rows, at[r]], there, out_ls).start()
                remote(out.at[other_rows, at[r]], there, out_ss, out_rs, other_core).start()
            if oa == 0:
                for r in both:
                    total = gp[:, at[r]].astype(F32)
                    for k in range(2):
                        src = r1.at[r, k, :, here]
                        remote(src, src, p1_ss, p1_rs.at[r, k, ob], later).wait_recv()
                        total += src[...].astype(F32)

                    @pl.when(ob == 0)
                    def _():
                        tot[r] = total

                    @pl.when(ob != 0)
                    def _():
                        gp[:, at[r]] = total.astype(BF)
                        remote(
                            gp.at[:, at[r]], r2.at[r, ob - 1], p2_ss, p2_rs.at[r, ob - 1], along(r, ob, True)).start()

    for n in range(4):
        blocks(n)

    def summed(r):
        total = tot[r]
        for k in range(3):
            remote(r2.at[r, k], r2.at[r, k], p2_ss, p2_rs.at[r, k], later).wait_recv()
            total += r2[r, k].astype(F32)
        return total

    send3[...] = summed(1).astype(BF)
    across = remote(send3, r3, p3_ss, p3_rs, dev(dx=1))
    across.start()
    total = summed(0)
    across.wait()
    wg[...] = (total + r3[...].astype(F32)).T.astype(BF)

    there = own.at[other_rows, :]
    remote(there, there, own_ss, own_rs, other_core).wait_send()
    remote(oth, oth, ex_ss, ex_rs.at[0, 0], later).wait_send()
    ref = gp.at[top, pl.ds(0, 16 * BLK)]
    remote(ref, ref, p0_ss, p0_rs.at[0, 0, 0], later).wait_send()
    ref = gp.at[:, pl.ds(0, 16 * BLK)]
    remote(ref, ref, p1_ss, p1_rs.at[0, 0, 0], later).wait_send()
    ref = gp.at[:, pl.ds(0, 6 * BLK)]
    remote(ref, ref, p2_ss, p2_rs.at[0, 0], later).wait_send()
    half = out.at[my_rows, :]
    pltpu.make_async_copy(half, half, out_ls).wait()
    remote(half, half, out_ss, out_rs, other_core).wait()


def per_device(section_feeds, adapter_weights):
    shard = adapter_weights[0]
    feed = section_feeds[0].reshape(ROWS, D)
    dma = pltpu.SemaphoreType.DMA
    vm = pltpu.VMEM
    res, wg = pl.pallas_call(
        kernel,
        out_shape=(jax.ShapeDtypeStruct((ROWS, D), BF), jax.ShapeDtypeStruct((BLK, 2 * RANK), BF)),
        in_specs=[pl.BlockSpec(memory_space=pl.ANY), pl.BlockSpec(memory_space=pltpu.VMEM)],
        out_specs=(pl.BlockSpec(memory_space=pl.ANY), pl.BlockSpec(memory_space=pltpu.VMEM)),
        scratch_shapes=[
            vm((2 * ROWS, HALF), BF), vm((2 * ROWS, HALF), BF), vm((3 * RANK, HALF), BF),
            vm((2 * ROWS, HALF), BF), vm((2 * RANK, HALF), BF),
            vm((2, 2, RANK, RING), BF), vm((2, 2, 2 * RANK, RING), BF), vm((2, 3, 2 * RANK, BLK), BF),
            vm((2, 2 * RANK, BLK), F32), vm((2 * RANK, BLK), BF), vm((2 * RANK, BLK), BF),
            vm((3, 2 * ROWS, RANK), F32), vm((2, RANK, RANK), F32), vm((2 * ROWS, 128), F32),
            vm((3, ROWS, RANK), F32), vm((2, RANK, RANK), F32), vm((ROWS, 128), F32),
            vm((2, ROWS, RANK), F32), vm((2, ROWS, RANK), F32),
            vm((4, 2 * ROWS, RANK), BF), vm((2, 2 * ROWS, 128), F32), vm((2, RANK, 2 * ROWS), BF),
            dma, dma, dma, dma, dma((16, 2)), dma((3,)), dma((3,)),
            dma((2, 5, 4)), dma((2, 5, 4)), dma((2, 2)), dma((16,)), dma((16,)), dma((5,)), dma((5,)), dma, dma, dma((4,)), dma((4,)),
            dma, dma((2, 2, 4)), dma, dma((2, 2, 4)), dma, dma((2, 3)), dma, dma, dma, dma, dma,
        ],
        compiler_params=pltpu.CompilerParams(
            collective_id=0, has_side_effects=True, vmem_limit_bytes=60 * 2**20),
        cost_estimate=pl.CostEstimate(flops=8 * 10**9, bytes_accessed=10**7, transcendentals=0),
        name="relay",
    )(feed, shard)
    return res.reshape(section_feeds.shape), wg[None]


def solution(mesh):
    placed = (P("section", None, "fsdp", None), P("section", "fsdp", None))
    return jax.shard_map(per_device, mesh=mesh, in_specs=placed, out_specs=placed, check_vma=False)
```

```python
import jax
import jax.numpy as jnp
from jax import lax
from jax.experimental import pallas as pl
from jax.experimental.pallas import tpu as pltpu
from jax.sharding import PartitionSpec as P

MESH = pl.DeviceIdType.MESH
EPSILON = 1e-05
BF = jnp.bfloat16
F32 = jnp.float32
NT = (((1,), (1,)), ((), ()))
NN = (((1,), (0,)), ((), ()))
D = 16384
RANK = 192
ROWS = 128
HALF = D // 2
BLK = 256
RING = 4 * BLK
PACE = ((2, 4, 5, 6, 7, 8, 9), (2, 4, 5, 5, 6, 7, 8, 9))
FROM_BACK = (2, 3, 1, 0)


def dot(a, b, dims):
    return lax.dot_general(a, b, dims, preferred_element_type=F32)


def dot_wide(a, b, dims):
    high = b.astype(BF)
    low = (b - high.astype(F32)).astype(BF)
    return dot(a, high, dims) + dot(a, low, dims)


def away(i):
    return lax.rem(2 + (i * (i + 1)) // 2, 4)


def kernel(
    feed, shard, res, wg,
    own, oth, w, out, gp, r0, r1, r2, tot, send3, r3,
    part, gram, sq, got_part, got_gram, got_sq, sg, got_sg, lr, bg, lrt,
    own_ss, own_rs, own_ls, ex_ss, ex_rs, pre_ss, pre_rs,
    ag_ss, ag_rs, own_part_ss, ship_ss, ship_rs, core_ss, core_rs, sg_ss, sg_rs, lr_ss, lr_rs,
    p0_ss, p0_rs, p1_ss, p1_rs, p2_ss, p2_rs, p3_ss, p3_rs, out_ss, out_rs, out_ls,
):
    s = lax.axis_index("section")
    f = lax.axis_index("fsdp")
    c = lax.rem(f, 2)
    xh = lax.rem(f // 2, 2)
    y = lax.rem(f // 4, 4)
    z = f // 16

    def dev(ss=0, dx=0, dy=0, dz=0, dc=0):
        sx = lax.rem(s + ss, 2)
        at = (lax.rem(z + dz, 4) * 4 + lax.rem(y + dy, 4)) * 2 + lax.rem(xh + dx, 2)
        return (sx, at * 2 + lax.rem(c + dc, 2))

    def remote(src, dst, ssem, rsem, to):
        return pltpu.make_async_remote_copy(
            src_ref=src, dst_ref=dst, send_sem=ssem, recv_sem=rsem,
            device_id=to, device_id_type=MESH)

    other_core, later = dev(dc=1), dev(ss=1)

    def turned(r, core):
        return lax.rem(r + core, 2)

    def place(r, oa, ob, core=c):
        q = turned(r, core)
        pa, pb = y * (1 - q) + z * q, z * (1 - q) + y * q
        return lax.rem(pa + oa, 4), lax.rem(pb + ob, 4)

    def block(r, a, b):
        return pl.ds(pl.multiple_of(((r * 4 + a) * 4 + b) * BLK, BLK), BLK)

    def lanes(r, oa, ob):
        return block(r, *place(r, oa, ob))

    def group_lanes(r, oa):
        a, _ = place(r, oa, 0)
        return pl.ds(pl.multiple_of((r * 4 + a) * RING, RING), RING)

    def feed_at(r, a, b, core):
        q = turned(r, core)
        jj = (b * (1 - q) + a * q) * 4 + a * (1 - q) + b * q
        return pl.ds(pl.multiple_of(((jj * 2 + lax.rem(xh + r, 2)) * 2 + core) * BLK, BLK), BLK)

    def along(r, d, second):
        q = turned(r + int(second), c)
        return dev(dy=d * (1 - q), dz=d * q)

    peers = [dict(dc=1), dict(ss=1), dict(ss=1, dc=1), dict(dx=1), dict(ss=1, dx=1)]
    peers += [dict(dy=d) for d in (1, 2, 3)] + [dict(dz=d) for d in (1, 2, 3)]
    barrier = pltpu.get_barrier_semaphore()
    for peer in peers:
        pl.semaphore_signal(barrier, inc=1, device_id=dev(**peer), device_id_type=MESH)
    turned_shard = shard[...].astype(F32).T.astype(BF)

    @pl.when(s == 0)
    def _():
        w[pl.ds(0, RANK), lanes(0, 0, 0)] = turned_shard[RANK:]
        w[pl.ds(RANK, RANK), lanes(0, 0, 0)] = turned_shard[:RANK]

    @pl.when(s == 1)
    def _():
        w[pl.ds(2 * RANK, RANK), lanes(0, 0, 0)] = turned_shard[:RANK]
        w[pl.ds(RANK, RANK), lanes(0, 0, 0)] = turned_shard[RANK:]

    pl.semaphore_wait(barrier, len(peers))

    my_rows = pl.ds(pl.multiple_of(c * ROWS, ROWS), ROWS)
    other_rows = pl.ds(pl.multiple_of((1 - c) * ROWS, ROWS), ROWS)

    def exchange(i):
        for r in range(2):
            oa, ob = away(i // 4), away(lax.rem(i, 4))
            for dc in range(2):
                core = lax.rem(c + dc, 2)
                a, b = place(r, oa, ob, core)
                remote(
                    feed.at[:, feed_at(r, a, b, core)], oth.at[my_rows, block(r, a, b)],
                    ex_ss, ex_rs.at[i, r], dev(ss=1, dc=dc)).start()

    def fill():
        @pl.loop(0, 32)
        def _(k):
            r, a, b = k // 16, lax.rem(k // 4, 4), lax.rem(k, 4)
            at = pl.ds(pl.multiple_of(k * BLK, BLK), BLK)
            remote(feed.at[:, feed_at(r, a, b, 1 - c)], own.at[my_rows, at], own_ss, own_rs, other_core).start()
            pltpu.make_async_copy(feed.at[:, feed_at(r, a, b, c)], own.at[my_rows, at], own_ls).start()

    def filled():
        whole = own.at[my_rows, :]
        pltpu.make_async_copy(whole, whole, own_ls).wait()
        there = own.at[other_rows, :]
        remote(there, there, own_ss, own_rs, other_core).wait_recv()

    from_later = [remote(sg.at[m], got_sg.at[m], sg_ss.at[m], sg_rs.at[m], later) for m in range(2)]

    def gather(section):
        rows = [(0, 3 * RANK), (0, 2 * RANK) if section == 0 else (RANK, RANK)]
        halves = [(pl.ds(start, n // 2), pl.ds(start + n // 2, n // 2)) for start, n in rows]
        begun = 0
        points = iter(PACE[section])

        def pace():
            nonlocal begun
            upto = next(points)
            if upto > begun:
                pl.loop(begun, upto)(exchange)
            begun = upto

        near, far = lanes(0, 0, 0), lanes(1, 0, 0)
        first, both = pl.ds(0, RANK), pl.ds(0, 2 * RANK)
        middle, last = pl.ds(RANK, RANK), pl.ds(2 * RANK, RANK)
        sent, kept = (first, both) if section == 0 else (last, middle)
        got = last if section == 0 else first
        diagonal = dev(ss=1, dx=1)
        pre = [
            remote(w.at[sent, near], w.at[sent, near], pre_ss.at[0], pre_rs.at[0], later),
            remote(w.at[kept, near], w.at[kept, far], pre_ss.at[2], pre_rs.at[2], dev(dx=1)),
        ]
        for copy in pre:
            copy.start()

        def arrived(rows, at, k):
            remote(w.at[rows, at], w.at[rows, at], pre_ss.at[k], pre_rs.at[k], later).wait_recv()

        def spot(r, oa, ob, part_rows=None):
            return w.at[pl.ds(*rows[r]) if part_rows is None else part_rows, lanes(r, oa % 4, ob % 4)]

        started = list(pre)

        def go(ref, r, g, k, to, sem=None):
            copy = remote(ref, ref, ag_ss.at[r, g, k] if sem is None else sem, ag_rs.at[r, g, k], to)
            copy.start()
            started.append(copy)

        def came(ref, r, g, k):
            remote(ref, ref, ag_ss.at[r, g, k], ag_rs.at[r, g, k], later).wait_recv()

        order = (0, -1, 1, 2)

        def ship(oa, ob):
            a, b = place(0, oa % 4, ob % 4)
            copy = remote(
                w.at[sent, block(0, a, b)], w.at[sent, block(1, b, a)], ship_ss.at[a * 4 + b], ship_rs.at[b * 4 + a],
                diagonal)
            copy.start()
            started.append(copy)

        def group_sends(r, g):
            for k, d in ((0, 1), (1, 3)):
                go(spot(r, order[g - 1], 0), r, g, k, along(r, d, True))

        def first_sends(r):
            for k, d in ((0, 1), (1, 3)):
                go(spot(r, 0, 0), r, 0, k, along(r, d, False))
            group_sends(r, 1)

        def forward(r, g):
            oa = order[g - 1]
            for k, d in ((0, -1), (1, 1)):
                came(spot(r, oa, d), r, g, k)
                go(spot(r, oa, d, halves[r][k]), r, g, 2 + k, along(r, -d % 4, True))
                if r == 0:
                    ship(oa, d)

        def complete(r, g):
            oa = order[g - 1]
            came(spot(r, oa, 2, halves[r][0]), r, g, 2)
            came(spot(r, oa, 2, halves[r][1]), r, g, 3)
            if r == 0:
                ship(oa, 2)

        def products(g):
            for r in range(2):
                at = group_lanes(r, order[g - 1] % 4)
                x = own[:, at]
                wide = section == 0 and r == 0
                for m in range(3 if wide else 2) if section == 0 or r == 0 else (1,):
                    part[m] += dot(x, w[pl.ds(m * RANK, RANK), at], NT)
                if section == 0:
                    u = w[pl.ds(0, RANK), at]
                    gram[0] += dot(u, u, NT)
                    if wide:
                        gram[1] += dot(u, w[last, at], NT)
                    xf = x.astype(F32)
                    sq[...] += jnp.broadcast_to(jnp.sum(xf * xf, axis=1, keepdims=True), sq.shape)

        def far_products():
            for k in range(16):
                ref = w.at[got, pl.ds((16 + k) * BLK, BLK)]
                remote(ref, ref, ship_ss.at[0], ship_rs.at[k], diagonal).wait_recv()

            @pl.loop(0, 4)
            def _(k):
                at = pl.ds(pl.multiple_of((4 + k) * RING, RING), RING)
                part[2 if section == 0 else 0] += dot(own[:, at], w[got, at], NT)
                if section == 0:
                    gram[1] += dot(w[pl.ds(0, RANK), at], w[last, at], NT)

        local = both if section == 0 else pl.ds(RANK, 2 * RANK)
        for rows_now, sem in ((local, own_part_ss), (got, None)):
            if sem is None:
                ship(0, 0)
                pace()
                arrived(got, near, 0)
            for second in (False, True):
                for k, d in ((0, 1), (1, 3)):
                    go(spot(0, 0, 0, rows_now), 0, int(second), k, along(0, d, second),
                       None if sem is None else sem.at[int(second), k])
        arrived(kept, far, 2)
        first_sends(1)
        fill()
        part[...] = jnp.zeros_like(part)
        if section == 0:
            gram[...] = jnp.zeros_like(gram)
            sq[...] = jnp.zeros_like(sq)
        for r in range(2):
            for k, d in ((0, -1), (1, 1)):
                came(spot(r, d, 0), r, 0, k)
                go(spot(r, d, 0, halves[r][k]), r, 0, 2 + k, along(r, -d % 4, False))
                group_sends(r, 2 + k)
                if r == 0:
                    ship(d, 0)
        pace()
        for r in range(2):
            forward(r, 1)
        for r in range(2):
            came(spot(r, 2, 0, halves[r][0]), r, 0, 2)
            came(spot(r, 2, 0, halves[r][1]), r, 0, 3)
            group_sends(r, 4)
            if r == 0:
                ship(2, 0)
        pace()
        filled()
        for g in (2, 3, 4):
            for r in range(2):
                forward(r, g)
            pace()
            if g == 3:
                for r in range(2):
                    complete(r, 1)
                products(1)
        for g in (2, 3):
            for r in range(2):
                complete(r, g)
            products(g)
        for r in range(2):
            complete(r, 4)
        pace()
        products(4)

        def to_core(src, dst, k):
            copy = remote(src, dst, core_ss.at[k], core_rs.at[k], other_core)
            copy.start()
            return copy

        if section == 0:
            two, third = pl.ds(0, 2), pl.ds(2, 1)
            handed = [
                to_core(part.at[two, other_rows], got_part.at[two], 0),
                to_core(gram.at[0], got_gram.at[0], 1),
                to_core(sq.at[other_rows], got_sq, 2),
            ]
            far_products()
            handed.append(to_core(part.at[third, other_rows], got_part.at[third], 3))
            handed.append(to_core(gram.at[1], got_gram.at[1], 4))
            for copy in handed:
                copy.wait()
        else:
            for m, k in ((1, 0), (0, 3)):
                if m == 0:
                    pace()
                    far_products()
                to_core(part.at[pl.ds(m, 1), other_rows], got_part.at[pl.ds(m, 1)], k).wait()
                sg[m] = part[m, my_rows] + got_part[m]
                from_later[m].start()
        return begun, started

    lr_mine, lr_other = lr.at[:, my_rows], lr.at[:, other_rows]
    bg_mine, bg_other = bg.at[:, my_rows], bg.at[:, other_rows]
    three = lr.at[pl.ds(0, 3), my_rows]
    three_other = lr.at[pl.ds(0, 3), other_rows]

    @pl.when(s == 1)
    def _():
        begun, started = gather(1)
        pl.loop(begun, 16)(exchange)
        for copy in from_later:
            copy.wait_send()
        remote(three, three, lr_ss.at[0], lr_rs.at[0], later).wait_recv()
        hand_on = remote(three, three, lr_ss.at[1], lr_rs.at[1], other_core)
        hand_on.start()
        remote(three_other, three_other, lr_ss.at[1], lr_rs.at[1], other_core).wait_recv()
        hand_on.wait_send()
        for copy in started:
            copy.wait_send()
        lrt[0] = lr[1].astype(F32).T.astype(BF)
        lrt[1] = lr[2].astype(F32).T.astype(BF)

    @pl.when(s == 0)
    def _():
        begun, started = gather(0)
        q0, p0, r = [part[m, my_rows] + got_part[m] for m in range(3)]
        uu = gram[0] + got_gram[0]
        ua = gram[1] + got_gram[1]
        sx = (sq[my_rows] + got_sq[...])[:, :1]
        inv0 = lax.rsqrt(sx * (1.0 / D) + EPSILON)
        pre0 = p0 * inv0
        sig0 = 1.0 / (1.0 + jnp.exp(-pre0))
        act0 = (pre0 * sig0).astype(BF)
        act0f = act0.astype(F32)
        t = dot_wide(act0, uu, NN)
        sb = sx + jnp.sum(act0f * (2.0 * q0 + t), axis=1, keepdims=True)
        inv1 = lax.rsqrt(jnp.maximum(sb, 0.0) * (1.0 / D) + EPSILON)
        p1 = r + dot_wide(act0, ua, NN)
        pre1 = p1 * inv1
        sig1 = 1.0 / (1.0 + jnp.exp(-pre1))
        act1 = (pre1 * sig1).astype(BF)
        from_later[1].wait_recv()
        pg1 = (got_sg[1] * sig1 * (1.0 + pre1 * (1.0 - sig1))).astype(BF).astype(F32)
        pg1s = (pg1 * inv1).astype(BF)
        lr[0, my_rows] = act0
        lr[1, my_rows] = pg1s
        lr[2, my_rows] = act1
        to_later = remote(three, three, lr_ss.at[0], lr_rs.at[0], later)
        to_later.start()
        pl.loop(begun, 16)(exchange)
        beta = inv1 * inv1 * inv1 * (jnp.sum(pg1 * p1, axis=1, keepdims=True) * (1.0 / D))
        from_later[0].wait_recv()
        ag0 = got_sg[0] + dot_wide(pg1s, ua, NT) - beta * (q0 + t)
        pg0 = (ag0 * sig0 * (1.0 + pre0 * (1.0 - sig0))).astype(BF).astype(F32)
        gamma = inv0 * inv0 * inv0 * (jnp.sum(pg0 * p0, axis=1, keepdims=True) * (1.0 / D))
        lr[3, my_rows] = (pg0 * inv0).astype(BF)
        bg[0, my_rows] = jnp.broadcast_to(beta, (ROWS, 128))
        bg[1, my_rows] = jnp.broadcast_to(gamma, (ROWS, 128))
        to_other = [
            remote(lr_mine, lr_mine, lr_ss.at[2], lr_rs.at[2], other_core),
            remote(bg_mine, bg_mine, lr_ss.at[3], lr_rs.at[3], other_core),
        ]
        for copy in to_other:
            copy.start()
        remote(lr_other, lr_other, lr_ss.at[2], lr_rs.at[2], other_core).wait_recv()
        remote(bg_other, bg_other, lr_ss.at[3], lr_rs.at[3], other_core).wait_recv()
        for copy in to_other + started:
            copy.wait_send()
        lrt[0] = lr[3].astype(F32).T.astype(BF)
        lrt[1] = lr[0].astype(F32).T.astype(BF)
        to_later.wait_send()

    top, bottom = pl.ds(0, RANK), pl.ds(RANK, RANK)

    def blocks(n):
        oa = FROM_BACK[n]

        @pl.loop(0, 4)
        def _(j):
            ob = away(j)
            here = pl.ds(pl.multiple_of(ob * BLK, BLK), BLK)
            both = range(2)
            at = [lanes(r, oa, ob) for r in both]
            for r in both:
                new = oth.at[:, at[r]]
                remote(new, new, ex_ss, ex_rs.at[n * 4 + j, r], later).wait_recv()
                if oa in (1, 3):
                    k = oa // 2
                    src = r0.at[r, k, :, here]
                    remote(src, src, p0_ss, p0_rs.at[r, k, ob], later).wait_recv()

            def store(done, down, up):
                if oa == 1:
                    down = [down[r] + r0[r, 0, :, here].astype(F32) for r in both]
                if oa == 3:
                    up = [up[r] + r0[r, 1, :, here].astype(F32) for r in both]
                for r in both:
                    out[:, at[r]] = done[r]
                    gp[top, at[r]] = down[r].astype(BF)
                    gp[bottom, at[r]] = up[r].astype(BF)

            @pl.when(s == 0)
            def _():
                x, g = [own[:, at[r]] for r in both], [oth[:, at[r]] for r in both]
                xf = [x[r].astype(F32) for r in both]
                beta = bg[0][:, :1]
                gamma = bg[1][:, :1]
                grown = [dot(lr[0], w[pl.ds(0, RANK), at[r]], NN) for r in both]
                slope = [dot(lr[1], w[pl.ds(2 * RANK, RANK), at[r]], NN) for r in both]
                bound = [(xf[r] + grown[r]).astype(BF).astype(F32) for r in both]
                passed = [(g[r].astype(F32) + slope[r] - beta * bound[r]).astype(BF) for r in both]
                first = [dot(lr[3], w[pl.ds(RANK, RANK), at[r]], NN) for r in both]
                down = [dot(lrt[0], x[r], NN) for r in both]
                up = [dot(lrt[1], passed[r], NN) for r in both]
                done = [(passed[r].astype(F32) + first[r] - gamma * xf[r]).astype(BF) for r in both]
                store(done, down, up)

            @pl.when(s == 1)
            def _():
                x, g = [oth[:, at[r]] for r in both], [own[:, at[r]] for r in both]
                grown = [dot(lr[0], w[pl.ds(0, RANK), at[r]], NN) for r in both]
                final = [dot(lr[2], w[pl.ds(RANK, RANK), at[r]], NN) for r in both]
                up = [dot(lrt[1], g[r], NN) for r in both]
                bound = [(x[r].astype(F32) + grown[r]).astype(BF) for r in both]
                down = [dot(lrt[0], bound[r], NN) for r in both]
                done = [(bound[r].astype(F32) + final[r]).astype(BF) for r in both]
                store(done, down, up)

            for r in both:
                if oa == 2:
                    for k, rows, d in ((0, top, 1), (1, bottom, 3)):
                        remote(
                            gp.at[rows, at[r]], r0.at[r, k, :, here], p0_ss, p0_rs.at[r, k, ob],
                            along(r, d, False)).start()
                elif oa:
                    k = oa // 2
                    remote(
                        gp.at[:, at[r]], r1.at[r, k, :, here], p1_ss, p1_rs.at[r, k, ob], along(r, oa, False)).start()
            for r in both:
                there = res.at[:, feed_at(r, *place(r, oa, ob), c)]
                pltpu.make_async_copy(out.at[my_rows, at[r]], there, out_ls).start()
                remote(out.at[other_rows, at[r]], there, out_ss, out_rs, other_core).start()
            if oa == 0:
                for r in both:
                    total = gp[:, at[r]].astype(F32)
                    for k in range(2):
                        src = r1.at[r, k, :, here]
                        remote(src, src, p1_ss, p1_rs.at[r, k, ob], later).wait_recv()
                        total += src[...].astype(F32)

                    @pl.when(ob == 0)
                    def _():
                        tot[r] = total

                    @pl.when(ob != 0)
                    def _():
                        gp[:, at[r]] = total.astype(BF)
                        remote(
                            gp.at[:, at[r]], r2.at[r, ob - 1], p2_ss, p2_rs.at[r, ob - 1], along(r, ob, True)).start()

    for n in range(4):
        blocks(n)

    def summed(r):
        total = tot[r]
        for k in range(3):
            remote(r2.at[r, k], r2.at[r, k], p2_ss, p2_rs.at[r, k], later).wait_recv()
            total += r2[r, k].astype(F32)
        return total

    send3[...] = summed(1).astype(BF)
    across = remote(send3, r3, p3_ss, p3_rs, dev(dx=1))
    across.start()
    total = summed(0)
    across.wait()
    wg[...] = (total + r3[...].astype(F32)).T.astype(BF)

    there = own.at[other_rows, :]
    remote(there, there, own_ss, own_rs, other_core).wait_send()
    remote(oth, oth, ex_ss, ex_rs.at[0, 0], later).wait_send()
    ref = gp.at[top, pl.ds(0, 16 * BLK)]
    remote(ref, ref, p0_ss, p0_rs.at[0, 0, 0], later).wait_send()
    ref = gp.at[:, pl.ds(0, 16 * BLK)]
    remote(ref, ref, p1_ss, p1_rs.at[0, 0, 0], later).wait_send()
    ref = gp.at[:, pl.ds(0, 6 * BLK)]
    remote(ref, ref, p2_ss, p2_rs.at[0, 0], later).wait_send()
    half = out.at[my_rows, :]
    pltpu.make_async_copy(half, half, out_ls).wait()
    remote(half, half, out_ss, out_rs, other_core).wait()


def per_device(section_feeds, adapter_weights):
    shard = adapter_weights[0]
    feed = section_feeds[0].reshape(ROWS, D)
    dma = pltpu.SemaphoreType.DMA
    vm = pltpu.VMEM
    res, wg = pl.pallas_call(
        kernel,
        out_shape=(jax.ShapeDtypeStruct((ROWS, D), BF), jax.ShapeDtypeStruct((BLK, 2 * RANK), BF)),
        in_specs=[pl.BlockSpec(memory_space=pl.ANY), pl.BlockSpec(memory_space=pltpu.VMEM)],
        out_specs=(pl.BlockSpec(memory_space=pl.ANY), pl.BlockSpec(memory_space=pltpu.VMEM)),
        scratch_shapes=[
            vm((2 * ROWS, HALF), BF), vm((2 * ROWS, HALF), BF), vm((3 * RANK, HALF), BF),
            vm((2 * ROWS, HALF), BF), vm((2 * RANK, HALF), BF),
            vm((2, 2, RANK, RING), BF), vm((2, 2, 2 * RANK, RING), BF), vm((2, 3, 2 * RANK, BLK), BF),
            vm((2, 2 * RANK, BLK), F32), vm((2 * RANK, BLK), BF), vm((2 * RANK, BLK), BF),
            vm((3, 2 * ROWS, RANK), F32), vm((2, RANK, RANK), F32), vm((2 * ROWS, 128), F32),
            vm((3, ROWS, RANK), F32), vm((2, RANK, RANK), F32), vm((ROWS, 128), F32),
            vm((2, ROWS, RANK), F32), vm((2, ROWS, RANK), F32),
            vm((4, 2 * ROWS, RANK), BF), vm((2, 2 * ROWS, 128), F32), vm((2, RANK, 2 * ROWS), BF),
            dma, dma, dma, dma, dma((16, 2)), dma((3,)), dma((3,)),
            dma((2, 5, 4)), dma((2, 5, 4)), dma((2, 2)), dma((16,)), dma((16,)), dma((5,)), dma((5,)), dma((2,)), dma((2,)), dma((4,)), dma((4,)),
            dma, dma((2, 2, 4)), dma, dma((2, 2, 4)), dma, dma((2, 3)), dma, dma, dma, dma, dma,
        ],
        compiler_params=pltpu.CompilerParams(
            collective_id=0, has_side_effects=True, vmem_limit_bytes=60 * 2**20),
        cost_estimate=pl.CostEstimate(flops=8 * 10**9, bytes_accessed=10**7, transcendentals=0),
        name="relay",
    )(feed, shard)
    return res.reshape(section_feeds.shape), wg[None]


def solution(mesh):
    placed = (P("section", None, "fsdp", None), P("section", "fsdp", None))
    return jax.shard_map(per_device, mesh=mesh, in_specs=placed, out_specs=placed, check_vma=False)
```

```python
import jax
import jax.numpy as jnp
from jax import lax
from jax.experimental import pallas as pl
from jax.experimental.pallas import tpu as pltpu
from jax.sharding import PartitionSpec as P

MESH = pl.DeviceIdType.MESH
EPSILON = 1e-05
BF = jnp.bfloat16
F32 = jnp.float32
NT = (((1,), (1,)), ((), ()))
NN = (((1,), (0,)), ((), ()))
D = 16384
RANK = 192
ROWS = 128
HALF = D // 2
BLK = 256
RING = 4 * BLK
PACE = ((4, 8, 10, 12, 14, 16, 18, 18), (4, 8, 10, 10, 12, 14, 16, 18))
FROM_BACK = (2, 3, 1, 0)


def dot(a, b, dims):
    return lax.dot_general(a, b, dims, preferred_element_type=F32)


def dot_wide(a, b, dims):
    high = b.astype(BF)
    low = (b - high.astype(F32)).astype(BF)
    return dot(a, high, dims) + dot(a, low, dims)


def away(i):
    return lax.rem(2 + (i * (i + 1)) // 2, 4)


def kernel(
    feed, shard, res, wg,
    own, oth, w, out, gp, r0, r1, r2, tot, send3, r3,
    part, gram, sq, got_part, got_gram, got_sq, sg, got_sg, lr, bg, lrt,
    own_ss, own_rs, own_ls, ex_ss, ex_rs, pre_ss, pre_rs,
    ag_ss, ag_rs, own_part_ss, ship_ss, ship_rs, core_ss, core_rs, sg_ss, sg_rs, lr_ss, lr_rs,
    p0_ss, p0_rs, p1_ss, p1_rs, p2_ss, p2_rs, p3_ss, p3_rs, out_ss, out_rs, out_ls,
):
    s = lax.axis_index("section")
    f = lax.axis_index("fsdp")
    c = lax.rem(f, 2)
    xh = lax.rem(f // 2, 2)
    y = lax.rem(f // 4, 4)
    z = f // 16

    def dev(ss=0, dx=0, dy=0, dz=0, dc=0):
        sx = lax.rem(s + ss, 2)
        at = (lax.rem(z + dz, 4) * 4 + lax.rem(y + dy, 4)) * 2 + lax.rem(xh + dx, 2)
        return (sx, at * 2 + lax.rem(c + dc, 2))

    def remote(src, dst, ssem, rsem, to):
        return pltpu.make_async_remote_copy(
            src_ref=src, dst_ref=dst, send_sem=ssem, recv_sem=rsem,
            device_id=to, device_id_type=MESH)

    other_core, later = dev(dc=1), dev(ss=1)

    def turned(r, core):
        return lax.rem(r + core, 2)

    def place(r, oa, ob, core=c):
        q = turned(r, core)
        pa, pb = y * (1 - q) + z * q, z * (1 - q) + y * q
        return lax.rem(pa + oa, 4), lax.rem(pb + ob, 4)

    def block(r, a, b):
        return pl.ds(pl.multiple_of(((r * 4 + a) * 4 + b) * BLK, BLK), BLK)

    def lanes(r, oa, ob):
        return block(r, *place(r, oa, ob))

    def group_lanes(r, oa):
        a, _ = place(r, oa, 0)
        return pl.ds(pl.multiple_of((r * 4 + a) * RING, RING), RING)

    def feed_at(r, a, b, core):
        q = turned(r, core)
        jj = (b * (1 - q) + a * q) * 4 + a * (1 - q) + b * q
        return pl.ds(pl.multiple_of(((jj * 2 + lax.rem(xh + r, 2)) * 2 + core) * BLK, BLK), BLK)

    def along(r, d, second):
        q = turned(r + int(second), c)
        return dev(dy=d * (1 - q), dz=d * q)

    peers = [dict(dc=1), dict(ss=1), dict(ss=1, dc=1), dict(dx=1), dict(ss=1, dx=1)]
    peers += [dict(dy=d) for d in (1, 2, 3)] + [dict(dz=d) for d in (1, 2, 3)]
    barrier = pltpu.get_barrier_semaphore()
    for peer in peers:
        pl.semaphore_signal(barrier, inc=1, device_id=dev(**peer), device_id_type=MESH)
    turned_shard = shard[...].astype(F32).T.astype(BF)

    @pl.when(s == 0)
    def _():
        w[pl.ds(0, RANK), lanes(0, 0, 0)] = turned_shard[RANK:]
        w[pl.ds(RANK, RANK), lanes(0, 0, 0)] = turned_shard[:RANK]

    @pl.when(s == 1)
    def _():
        w[pl.ds(2 * RANK, RANK), lanes(0, 0, 0)] = turned_shard[:RANK]
        w[pl.ds(RANK, RANK), lanes(0, 0, 0)] = turned_shard[RANK:]

    pl.semaphore_wait(barrier, len(peers))

    my_rows = pl.ds(pl.multiple_of(c * ROWS, ROWS), ROWS)
    other_rows = pl.ds(pl.multiple_of((1 - c) * ROWS, ROWS), ROWS)

    def exchange(k):
        late = k // 24
        i = (k // 2) * (1 - late) + (12 + lax.rem(k, 4)) * late
        r = lax.rem(k, 2) * (1 - late) + (7 - k // 4) * late
        oa, ob = away(i // 4), away(lax.rem(i, 4))
        for dc in range(2):
            core = lax.rem(c + dc, 2)
            a, b = place(r, oa, ob, core)
            remote(
                feed.at[:, feed_at(r, a, b, core)], oth.at[my_rows, block(r, a, b)],
                ex_ss, ex_rs.at[i, r], dev(ss=1, dc=dc)).start()

    def fill():
        @pl.loop(0, 32)
        def _(k):
            r, a, b = k // 16, lax.rem(k // 4, 4), lax.rem(k, 4)
            at = pl.ds(pl.multiple_of(k * BLK, BLK), BLK)
            remote(feed.at[:, feed_at(r, a, b, 1 - c)], own.at[my_rows, at], own_ss, own_rs, other_core).start()
            pltpu.make_async_copy(feed.at[:, feed_at(r, a, b, c)], own.at[my_rows, at], own_ls).start()

    def filled():
        whole = own.at[my_rows, :]
        pltpu.make_async_copy(whole, whole, own_ls).wait()
        there = own.at[other_rows, :]
        remote(there, there, own_ss, own_rs, other_core).wait_recv()

    from_later = [remote(sg.at[m], got_sg.at[m], sg_ss.at[m], sg_rs.at[m], later) for m in range(2)]

    def gather(section):
        rows = [(0, 3 * RANK), (0, 2 * RANK) if section == 0 else (RANK, RANK)]
        halves = [(pl.ds(start, n // 2), pl.ds(start + n // 2, n // 2)) for start, n in rows]
        begun = 0
        points = iter(PACE[section])

        def pace():
            nonlocal begun
            upto = next(points)
            if upto > begun:
                pl.loop(begun, upto)(exchange)
            begun = upto

        near, far = lanes(0, 0, 0), lanes(1, 0, 0)
        first, both = pl.ds(0, RANK), pl.ds(0, 2 * RANK)
        middle, last = pl.ds(RANK, RANK), pl.ds(2 * RANK, RANK)
        sent, kept = (first, both) if section == 0 else (last, middle)
        got = last if section == 0 else first
        diagonal = dev(ss=1, dx=1)
        pre = [
            remote(w.at[sent, near], w.at[sent, near], pre_ss.at[0], pre_rs.at[0], later),
            remote(w.at[kept, near], w.at[kept, far], pre_ss.at[2], pre_rs.at[2], dev(dx=1)),
        ]
        for copy in pre:
            copy.start()

        def arrived(rows, at, k):
            remote(w.at[rows, at], w.at[rows, at], pre_ss.at[k], pre_rs.at[k], later).wait_recv()

        def spot(r, oa, ob, part_rows=None):
            return w.at[pl.ds(*rows[r]) if part_rows is None else part_rows, lanes(r, oa % 4, ob % 4)]

        started = list(pre)

        def go(ref, r, g, k, to, sem=None):
            copy = remote(ref, ref, ag_ss.at[r, g, k] if sem is None else sem, ag_rs.at[r, g, k], to)
            copy.start()
            started.append(copy)

        def came(ref, r, g, k):
            remote(ref, ref, ag_ss.at[r, g, k], ag_rs.at[r, g, k], later).wait_recv()

        order = (0, -1, 1, 2)

        def ship(oa, ob):
            a, b = place(0, oa % 4, ob % 4)
            copy = remote(
                w.at[sent, block(0, a, b)], w.at[sent, block(1, b, a)], ship_ss.at[a * 4 + b], ship_rs.at[b * 4 + a],
                diagonal)
            copy.start()
            started.append(copy)

        def group_sends(r, g):
            for k, d in ((0, 1), (1, 3)):
                go(spot(r, order[g - 1], 0), r, g, k, along(r, d, True))

        def first_sends(r):
            for k, d in ((0, 1), (1, 3)):
                go(spot(r, 0, 0), r, 0, k, along(r, d, False))
            group_sends(r, 1)

        def forward(r, g):
            oa = order[g - 1]
            for k, d in ((0, -1), (1, 1)):
                came(spot(r, oa, d), r, g, k)
                go(spot(r, oa, d, halves[r][k]), r, g, 2 + k, along(r, -d % 4, True))
                if r == 0:
                    ship(oa, d)

        def complete(r, g):
            oa = order[g - 1]
            came(spot(r, oa, 2, halves[r][0]), r, g, 2)
            came(spot(r, oa, 2, halves[r][1]), r, g, 3)
            if r == 0:
                ship(oa, 2)

        def products(g):
            for r in range(2):
                at = group_lanes(r, order[g - 1] % 4)
                x = own[:, at]
                wide = section == 0 and r == 0
                for m in range(3 if wide else 2) if section == 0 or r == 0 else (1,):
                    part[m] += dot(x, w[pl.ds(m * RANK, RANK), at], NT)
                if section == 0:
                    u = w[pl.ds(0, RANK), at]
                    gram[0] += dot(u, u, NT)
                    if wide:
                        gram[1] += dot(u, w[last, at], NT)
                    xf = x.astype(F32)
                    sq[...] += jnp.broadcast_to(jnp.sum(xf * xf, axis=1, keepdims=True), sq.shape)

        def far_products():
            for k in range(16):
                ref = w.at[got, pl.ds((16 + k) * BLK, BLK)]
                remote(ref, ref, ship_ss.at[0], ship_rs.at[k], diagonal).wait_recv()

            @pl.loop(0, 4)
            def _(k):
                at = pl.ds(pl.multiple_of((4 + k) * RING, RING), RING)
                part[2 if section == 0 else 0] += dot(own[:, at], w[got, at], NT)
                if section == 0:
                    gram[1] += dot(w[pl.ds(0, RANK), at], w[last, at], NT)

        local = both if section == 0 else pl.ds(RANK, 2 * RANK)
        for rows_now, sem in ((local, own_part_ss), (got, None)):
            if sem is None:
                ship(0, 0)
                pace()
                arrived(got, near, 0)
            for second in (False, True):
                for k, d in ((0, 1), (1, 3)):
                    go(spot(0, 0, 0, rows_now), 0, int(second), k, along(0, d, second),
                       None if sem is None else sem.at[int(second), k])
        arrived(kept, far, 2)
        first_sends(1)
        fill()
        part[...] = jnp.zeros_like(part)
        if section == 0:
            gram[...] = jnp.zeros_like(gram)
            sq[...] = jnp.zeros_like(sq)
        for r in range(2):
            for k, d in ((0, -1), (1, 1)):
                came(spot(r, d, 0), r, 0, k)
                go(spot(r, d, 0, halves[r][k]), r, 0, 2 + k, along(r, -d % 4, False))
                group_sends(r, 2 + k)
                if r == 0:
                    ship(d, 0)
        pace()
        for r in range(2):
            forward(r, 1)
        for r in range(2):
            came(spot(r, 2, 0, halves[r][0]), r, 0, 2)
            came(spot(r, 2, 0, halves[r][1]), r, 0, 3)
            group_sends(r, 4)
            if r == 0:
                ship(2, 0)
        pace()
        filled()
        for g in (2, 3, 4):
            for r in range(2):
                forward(r, g)
            pace()
            if g == 3:
                for r in range(2):
                    complete(r, 1)
                products(1)
        for g in (2, 3):
            for r in range(2):
                complete(r, g)
            products(g)
        for r in range(2):
            complete(r, 4)
        pace()
        products(4)

        def to_core(src, dst, k):
            copy = remote(src, dst, core_ss.at[k], core_rs.at[k], other_core)
            copy.start()
            return copy

        if section == 0:
            two, third = pl.ds(0, 2), pl.ds(2, 1)
            handed = [
                to_core(part.at[two, other_rows], got_part.at[two], 0),
                to_core(gram.at[0], got_gram.at[0], 1),
                to_core(sq.at[other_rows], got_sq, 2),
            ]
            far_products()
            handed.append(to_core(part.at[third, other_rows], got_part.at[third], 3))
            handed.append(to_core(gram.at[1], got_gram.at[1], 4))
            for copy in handed:
                copy.wait()
            pace()
        else:
            for m, k in ((1, 0), (0, 3)):
                if m == 0:
                    pace()
                    far_products()
                to_core(part.at[pl.ds(m, 1), other_rows], got_part.at[pl.ds(m, 1)], k).wait()
                sg[m] = (part[m, my_rows] + got_part[m]).astype(BF)
                from_later[m].start()
        return begun, started

    lr_mine, lr_other = lr.at[:, my_rows], lr.at[:, other_rows]
    bg_mine, bg_other = bg.at[:, my_rows], bg.at[:, other_rows]
    three = lr.at[pl.ds(0, 3), my_rows]
    three_other = lr.at[pl.ds(0, 3), other_rows]

    @pl.when(s == 1)
    def _():
        begun, started = gather(1)
        pl.loop(begun, 32)(exchange)
        for copy in from_later:
            copy.wait_send()
        remote(three, three, lr_ss.at[0], lr_rs.at[0], later).wait_recv()
        hand_on = remote(three, three, lr_ss.at[1], lr_rs.at[1], other_core)
        hand_on.start()
        remote(three_other, three_other, lr_ss.at[1], lr_rs.at[1], other_core).wait_recv()
        hand_on.wait_send()
        for copy in started:
            copy.wait_send()
        lrt[0] = lr[1].astype(F32).T.astype(BF)
        lrt[1] = lr[2].astype(F32).T.astype(BF)

    @pl.when(s == 0)
    def _():
        begun, started = gather(0)
        q0, p0, r = [part[m, my_rows] + got_part[m] for m in range(3)]
        uu = gram[0] + got_gram[0]
        ua = gram[1] + got_gram[1]
        sx = (sq[my_rows] + got_sq[...])[:, :1]
        inv0 = lax.rsqrt(sx * (1.0 / D) + EPSILON)
        pre0 = p0 * inv0
        sig0 = 1.0 / (1.0 + jnp.exp(-pre0))
        act0 = (pre0 * sig0).astype(BF)
        act0f = act0.astype(F32)
        t = dot_wide(act0, uu, NN)
        sb = sx + jnp.sum(act0f * (2.0 * q0 + t), axis=1, keepdims=True)
        inv1 = lax.rsqrt(jnp.maximum(sb, 0.0) * (1.0 / D) + EPSILON)
        p1 = r + dot_wide(act0, ua, NN)
        pre1 = p1 * inv1
        sig1 = 1.0 / (1.0 + jnp.exp(-pre1))
        act1 = (pre1 * sig1).astype(BF)
        from_later[1].wait_recv()
        pg1 = (got_sg[1].astype(F32) * sig1 * (1.0 + pre1 * (1.0 - sig1))).astype(BF).astype(F32)
        pg1s = (pg1 * inv1).astype(BF)
        lr[0, my_rows] = act0
        lr[1, my_rows] = pg1s
        lr[2, my_rows] = act1
        to_later = remote(three, three, lr_ss.at[0], lr_rs.at[0], later)
        to_later.start()
        pl.loop(begun, 32)(exchange)
        beta = inv1 * inv1 * inv1 * (jnp.sum(pg1 * p1, axis=1, keepdims=True) * (1.0 / D))
        from_later[0].wait_recv()
        ag0 = got_sg[0].astype(F32) + dot_wide(pg1s, ua, NT) - beta * (q0 + t)
        pg0 = (ag0 * sig0 * (1.0 + pre0 * (1.0 - sig0))).astype(BF).astype(F32)
        gamma = inv0 * inv0 * inv0 * (jnp.sum(pg0 * p0, axis=1, keepdims=True) * (1.0 / D))
        lr[3, my_rows] = (pg0 * inv0).astype(BF)
        bg[0, my_rows] = jnp.broadcast_to(beta, (ROWS, 128))
        bg[1, my_rows] = jnp.broadcast_to(gamma, (ROWS, 128))
        to_other = [
            remote(lr_mine, lr_mine, lr_ss.at[2], lr_rs.at[2], other_core),
            remote(bg_mine, bg_mine, lr_ss.at[3], lr_rs.at[3], other_core),
        ]
        for copy in to_other:
            copy.start()
        remote(lr_other, lr_other, lr_ss.at[2], lr_rs.at[2], other_core).wait_recv()
        remote(bg_other, bg_other, lr_ss.at[3], lr_rs.at[3], other_core).wait_recv()
        for copy in to_other + started:
            copy.wait_send()
        lrt[0] = lr[3].astype(F32).T.astype(BF)
        lrt[1] = lr[0].astype(F32).T.astype(BF)
        to_later.wait_send()

    top, bottom = pl.ds(0, RANK), pl.ds(RANK, RANK)

    def blocks(n, both=(1, 0), low=0, high=4):
        oa = FROM_BACK[n]

        @pl.loop(low, high)
        def _(j):
            ob = away(j)
            here = pl.ds(pl.multiple_of(ob * BLK, BLK), BLK)
            at = {r: lanes(r, oa, ob) for r in both}
            for r in both:
                new = oth.at[:, at[r]]
                remote(new, new, ex_ss, ex_rs.at[n * 4 + j, r], later).wait_recv()
                if oa in (1, 3):
                    k = oa // 2
                    src = r0.at[r, k, :, here]
                    remote(src, src, p0_ss, p0_rs.at[r, k, ob], later).wait_recv()

            def store(done, down, up):
                if oa == 1:
                    down = {r: down[r] + r0[r, 0, :, here].astype(F32) for r in both}
                if oa == 3:
                    up = {r: up[r] + r0[r, 1, :, here].astype(F32) for r in both}
                for r in both:
                    out[:, at[r]] = done[r]
                    gp[top, at[r]] = down[r].astype(BF)
                    gp[bottom, at[r]] = up[r].astype(BF)

            @pl.when(s == 0)
            def _():
                x, g = {r: own[:, at[r]] for r in both}, {r: oth[:, at[r]] for r in both}
                xf = {r: x[r].astype(F32) for r in both}
                beta = bg[0][:, :1]
                gamma = bg[1][:, :1]
                grown = {r: dot(lr[0], w[pl.ds(0, RANK), at[r]], NN) for r in both}
                slope = {r: dot(lr[1], w[pl.ds(2 * RANK, RANK), at[r]], NN) for r in both}
                bound = {r: (xf[r] + grown[r]).astype(BF).astype(F32) for r in both}
                passed = {r: (g[r].astype(F32) + slope[r] - beta * bound[r]).astype(BF) for r in both}
                first = {r: dot(lr[3], w[pl.ds(RANK, RANK), at[r]], NN) for r in both}
                down = {r: dot(lrt[0], x[r], NN) for r in both}
                up = {r: dot(lrt[1], passed[r], NN) for r in both}
                done = {r: (passed[r].astype(F32) + first[r] - gamma * xf[r]).astype(BF) for r in both}
                store(done, down, up)

            @pl.when(s == 1)
            def _():
                x, g = {r: oth[:, at[r]] for r in both}, {r: own[:, at[r]] for r in both}
                grown = {r: dot(lr[0], w[pl.ds(0, RANK), at[r]], NN) for r in both}
                final = {r: dot(lr[2], w[pl.ds(RANK, RANK), at[r]], NN) for r in both}
                up = {r: dot(lrt[1], g[r], NN) for r in both}
                bound = {r: (x[r].astype(F32) + grown[r]).astype(BF) for r in both}
                down = {r: dot(lrt[0], bound[r], NN) for r in both}
                done = {r: (bound[r].astype(F32) + final[r]).astype(BF) for r in both}
                store(done, down, up)

            for r in both:
                if oa == 2:
                    for k, rows, d in ((0, top, 1), (1, bottom, 3)):
                        remote(
                            gp.at[rows, at[r]], r0.at[r, k, :, here], p0_ss, p0_rs.at[r, k, ob],
                            along(r, d, False)).start()
                elif oa:
                    k = oa // 2
                    remote(
                        gp.at[:, at[r]], r1.at[r, k, :, here], p1_ss, p1_rs.at[r, k, ob], along(r, oa, False)).start()
            for r in both:
                there = res.at[:, feed_at(r, *place(r, oa, ob), c)]
                pltpu.make_async_copy(out.at[my_rows, at[r]], there, out_ls).start()
                remote(out.at[other_rows, at[r]], there, out_ss, out_rs, other_core).start()
            if oa == 0:
                for r in both:
                    total = gp[:, at[r]].astype(F32)
                    for k in range(2):
                        src = r1.at[r, k, :, here]
                        remote(src, src, p1_ss, p1_rs.at[r, k, ob], later).wait_recv()
                        total += src[...].astype(F32)

                    @pl.when(ob == 0)
                    def _():
                        tot[r] = total

                    @pl.when(ob != 0)
                    def _():
                        gp[:, at[r]] = total.astype(BF)
                        remote(
                            gp.at[:, at[r]], r2.at[r, ob - 1], p2_ss, p2_rs.at[r, ob - 1], along(r, ob, True)).start()

    def summed(r):
        total = tot[r]
        for k in range(3):
            remote(r2.at[r, k], r2.at[r, k], p2_ss, p2_rs.at[r, k], later).wait_recv()
            total += r2[r, k].astype(F32)
        return total

    for n in range(3):
        blocks(n)
    blocks(3, (1,))
    blocks(3, (0,), 0, 2)
    send3[...] = summed(1).astype(BF)
    across = remote(send3, r3, p3_ss, p3_rs, dev(dx=1))
    across.start()
    blocks(3, (0,), 2, 4)
    total = summed(0)
    across.wait()
    wg[...] = (total + r3[...].astype(F32)).T.astype(BF)

    there = own.at[other_rows, :]
    remote(there, there, own_ss, own_rs, other_core).wait_send()
    remote(oth, oth, ex_ss, ex_rs.at[0, 0], later).wait_send()
    ref = gp.at[top, pl.ds(0, 16 * BLK)]
    remote(ref, ref, p0_ss, p0_rs.at[0, 0, 0], later).wait_send()
    ref = gp.at[:, pl.ds(0, 16 * BLK)]
    remote(ref, ref, p1_ss, p1_rs.at[0, 0, 0], later).wait_send()
    ref = gp.at[:, pl.ds(0, 6 * BLK)]
    remote(ref, ref, p2_ss, p2_rs.at[0, 0], later).wait_send()
    half = out.at[my_rows, :]
    pltpu.make_async_copy(half, half, out_ls).wait()
    remote(half, half, out_ss, out_rs, other_core).wait()


def per_device(section_feeds, adapter_weights):
    shard = adapter_weights[0]
    feed = section_feeds[0].reshape(ROWS, D)
    dma = pltpu.SemaphoreType.DMA
    vm = pltpu.VMEM
    res, wg = pl.pallas_call(
        kernel,
        out_shape=(jax.ShapeDtypeStruct((ROWS, D), BF), jax.ShapeDtypeStruct((BLK, 2 * RANK), BF)),
        in_specs=[pl.BlockSpec(memory_space=pl.ANY), pl.BlockSpec(memory_space=pltpu.VMEM)],
        out_specs=(pl.BlockSpec(memory_space=pl.ANY), pl.BlockSpec(memory_space=pltpu.VMEM)),
        scratch_shapes=[
            vm((2 * ROWS, HALF), BF), vm((2 * ROWS, HALF), BF), vm((3 * RANK, HALF), BF),
            vm((2 * ROWS, HALF), BF), vm((2 * RANK, HALF), BF),
            vm((2, 2, RANK, RING), BF), vm((2, 2, 2 * RANK, RING), BF), vm((2, 3, 2 * RANK, BLK), BF),
            vm((2, 2 * RANK, BLK), F32), vm((2 * RANK, BLK), BF), vm((2 * RANK, BLK), BF),
            vm((3, 2 * ROWS, RANK), F32), vm((2, RANK, RANK), F32), vm((2 * ROWS, 128), F32),
            vm((3, ROWS, RANK), F32), vm((2, RANK, RANK), F32), vm((ROWS, 128), F32),
            vm((2, ROWS, RANK), BF), vm((2, ROWS, RANK), BF),
            vm((4, 2 * ROWS, RANK), BF), vm((2, 2 * ROWS, 128), F32), vm((2, RANK, 2 * ROWS), BF),
            dma, dma, dma, dma, dma((16, 2)), dma((3,)), dma((3,)),
            dma((2, 5, 4)), dma((2, 5, 4)), dma((2, 2)), dma((16,)), dma((16,)), dma((5,)), dma((5,)), dma((2,)), dma((2,)), dma((4,)), dma((4,)),
            dma, dma((2, 2, 4)), dma, dma((2, 2, 4)), dma, dma((2, 3)), dma, dma, dma, dma, dma,
        ],
        compiler_params=pltpu.CompilerParams(
            collective_id=0, has_side_effects=True, vmem_limit_bytes=60 * 2**20),
        cost_estimate=pl.CostEstimate(flops=8 * 10**9, bytes_accessed=10**7, transcendentals=0),
        name="relay",
    )(feed, shard)
    return res.reshape(section_feeds.shape), wg[None]


def solution(mesh):
    placed = (P("section", None, "fsdp", None), P("section", "fsdp", None))
    return jax.shard_map(per_device, mesh=mesh, in_specs=placed, out_specs=placed, check_vma=False)
```

```python
import jax
import jax.numpy as jnp
from jax import lax
from jax.experimental import pallas as pl
from jax.experimental.pallas import tpu as pltpu
from jax.sharding import PartitionSpec as P

MESH = pl.DeviceIdType.MESH
EPSILON = 1e-05
BF = jnp.bfloat16
F32 = jnp.float32
NT = (((1,), (1,)), ((), ()))
NN = (((1,), (0,)), ((), ()))
D = 16384
RANK = 192
ROWS = 128
HALF = D // 2
BLK = 256
RING = 4 * BLK
PACE = ((4, 8, 10, 12, 14, 16, 18, 18), (4, 8, 10, 10, 12, 14, 16, 18))
FROM_BACK = (2, 3, 1, 0)


def dot(a, b, dims):
    return lax.dot_general(a, b, dims, preferred_element_type=F32)


def dot_wide(a, b, dims):
    high = b.astype(BF)
    low = (b - high.astype(F32)).astype(BF)
    return dot(a, high, dims) + dot(a, low, dims)


def away(i):
    return lax.rem(2 + (i * (i + 1)) // 2, 4)


def kernel(
    feed, shard, res, wg,
    own, oth, w, out, gp, r0, r1, r2, tot, send3, r3,
    part, gram, sq, got_part, got_gram, got_sq, sg, got_sg, lr, bg, lrt,
    own_ss, own_rs, own_ls, ex_ss, ex_rs, pre_ss, pre_rs,
    ag_ss, ag_rs, own_part_ss, ship_ss, ship_rs, core_ss, core_rs, sg_ss, sg_rs, lr_ss, lr_rs,
    p0_ss, p0_rs, p1_ss, p1_rs, p2_ss, p2_rs, p3_ss, p3_rs, out_ss, out_rs, out_ls,
):
    s = lax.axis_index("section")
    f = lax.axis_index("fsdp")
    c = lax.rem(f, 2)
    xh = lax.rem(f // 2, 2)
    y = lax.rem(f // 4, 4)
    z = f // 16

    def dev(ss=0, dx=0, dy=0, dz=0, dc=0):
        sx = lax.rem(s + ss, 2)
        at = (lax.rem(z + dz, 4) * 4 + lax.rem(y + dy, 4)) * 2 + lax.rem(xh + dx, 2)
        return (sx, at * 2 + lax.rem(c + dc, 2))

    def remote(src, dst, ssem, rsem, to):
        return pltpu.make_async_remote_copy(
            src_ref=src, dst_ref=dst, send_sem=ssem, recv_sem=rsem,
            device_id=to, device_id_type=MESH)

    other_core, later = dev(dc=1), dev(ss=1)

    def turned(r, core):
        return lax.rem(r + core, 2)

    def place(r, oa, ob, core=c):
        q = turned(r, core)
        pa, pb = y * (1 - q) + z * q, z * (1 - q) + y * q
        return lax.rem(pa + oa, 4), lax.rem(pb + ob, 4)

    def block(r, a, b):
        return pl.ds(pl.multiple_of(((r * 4 + a) * 4 + b) * BLK, BLK), BLK)

    def lanes(r, oa, ob):
        return block(r, *place(r, oa, ob))

    def group_lanes(r, oa):
        a, _ = place(r, oa, 0)
        return pl.ds(pl.multiple_of((r * 4 + a) * RING, RING), RING)

    def feed_at(r, a, b, core):
        q = turned(r, core)
        jj = (b * (1 - q) + a * q) * 4 + a * (1 - q) + b * q
        return pl.ds(pl.multiple_of(((jj * 2 + lax.rem(xh + r, 2)) * 2 + core) * BLK, BLK), BLK)

    def along(r, d, second):
        q = turned(r + int(second), c)
        return dev(dy=d * (1 - q), dz=d * q)

    peers = [dict(dc=1), dict(ss=1), dict(ss=1, dc=1), dict(dx=1), dict(ss=1, dx=1)]
    peers += [dict(dy=d) for d in (1, 2, 3)] + [dict(dz=d) for d in (1, 2, 3)]
    barrier = pltpu.get_barrier_semaphore()
    for peer in peers:
        pl.semaphore_signal(barrier, inc=1, device_id=dev(**peer), device_id_type=MESH)
    turned_shard = shard[...].astype(F32).T.astype(BF)

    @pl.when(s == 0)
    def _():
        w[pl.ds(0, RANK), lanes(0, 0, 0)] = turned_shard[RANK:]
        w[pl.ds(RANK, RANK), lanes(0, 0, 0)] = turned_shard[:RANK]

    @pl.when(s == 1)
    def _():
        w[pl.ds(2 * RANK, RANK), lanes(0, 0, 0)] = turned_shard[:RANK]
        w[pl.ds(RANK, RANK), lanes(0, 0, 0)] = turned_shard[RANK:]

    pl.semaphore_wait(barrier, len(peers))

    my_rows = pl.ds(pl.multiple_of(c * ROWS, ROWS), ROWS)
    other_rows = pl.ds(pl.multiple_of((1 - c) * ROWS, ROWS), ROWS)

    def exchange(k):
        late = k // 24
        i = (k // 2) * (1 - late) + (12 + lax.rem(k, 4)) * late
        r = lax.rem(k, 2) * (1 - late) + (7 - k // 4) * late
        oa, ob = away(i // 4), away(lax.rem(i, 4))
        for dc in range(2):
            core = lax.rem(c + dc, 2)
            a, b = place(r, oa, ob, core)
            remote(
                feed.at[:, feed_at(r, a, b, core)], oth.at[my_rows, block(r, a, b)],
                ex_ss, ex_rs.at[i, r], dev(ss=1, dc=dc)).start()

    def fill():
        @pl.loop(0, 32)
        def _(k):
            r, a, b = k // 16, lax.rem(k // 4, 4), lax.rem(k, 4)
            at = pl.ds(pl.multiple_of(k * BLK, BLK), BLK)
            remote(feed.at[:, feed_at(r, a, b, 1 - c)], own.at[my_rows, at], own_ss, own_rs, other_core).start()
            pltpu.make_async_copy(feed.at[:, feed_at(r, a, b, c)], own.at[my_rows, at], own_ls).start()

    def filled():
        whole = own.at[my_rows, :]
        pltpu.make_async_copy(whole, whole, own_ls).wait()
        there = own.at[other_rows, :]
        remote(there, there, own_ss, own_rs, other_core).wait_recv()

    from_later = [remote(sg.at[m], got_sg.at[m], sg_ss.at[m], sg_rs.at[m], later) for m in range(2)]

    def gather(section):
        rows = [(0, 3 * RANK), (0, 2 * RANK) if section == 0 else (RANK, RANK)]
        halves = [(pl.ds(start, n // 2), pl.ds(start + n // 2, n // 2)) for start, n in rows]
        begun = 0
        points = iter(PACE[section])

        def pace():
            nonlocal begun
            upto = next(points)
            if upto > begun:
                pl.loop(begun, upto)(exchange)
            begun = upto

        near, far = lanes(0, 0, 0), lanes(1, 0, 0)
        first, both = pl.ds(0, RANK), pl.ds(0, 2 * RANK)
        middle, last = pl.ds(RANK, RANK), pl.ds(2 * RANK, RANK)
        sent, kept = (first, both) if section == 0 else (last, middle)
        got = last if section == 0 else first
        diagonal = dev(ss=1, dx=1)
        pre = [
            remote(w.at[sent, near], w.at[sent, near], pre_ss.at[0], pre_rs.at[0], later),
            remote(w.at[kept, near], w.at[kept, far], pre_ss.at[2], pre_rs.at[2], dev(dx=1)),
        ]
        for copy in pre:
            copy.start()

        def arrived(rows, at, k):
            remote(w.at[rows, at], w.at[rows, at], pre_ss.at[k], pre_rs.at[k], later).wait_recv()

        def spot(r, oa, ob, part_rows=None):
            return w.at[pl.ds(*rows[r]) if part_rows is None else part_rows, lanes(r, oa % 4, ob % 4)]

        started = list(pre)

        def go(ref, r, g, k, to, sem=None):
            copy = remote(ref, ref, ag_ss.at[r, g, k] if sem is None else sem, ag_rs.at[r, g, k], to)
            copy.start()
            started.append(copy)

        def came(ref, r, g, k):
            remote(ref, ref, ag_ss.at[r, g, k], ag_rs.at[r, g, k], later).wait_recv()

        order = (0, -1, 1, 2)

        def ship(oa, ob):
            a, b = place(0, oa % 4, ob % 4)
            copy = remote(
                w.at[sent, block(0, a, b)], w.at[sent, block(1, b, a)], ship_ss.at[a * 4 + b], ship_rs.at[b * 4 + a],
                diagonal)
            copy.start()
            started.append(copy)

        def group_sends(r, g):
            for k, d in ((0, 1), (1, 3)):
                go(spot(r, order[g - 1], 0), r, g, k, along(r, d, True))

        def first_sends(r):
            for k, d in ((0, 1), (1, 3)):
                go(spot(r, 0, 0), r, 0, k, along(r, d, False))
            group_sends(r, 1)

        def forward(r, g):
            oa = order[g - 1]
            for k, d in ((0, -1), (1, 1)):
                came(spot(r, oa, d), r, g, k)
                go(spot(r, oa, d, halves[r][k]), r, g, 2 + k, along(r, -d % 4, True))
                if r == 0:
                    ship(oa, d)

        def complete(r, g):
            oa = order[g - 1]
            came(spot(r, oa, 2, halves[r][0]), r, g, 2)
            came(spot(r, oa, 2, halves[r][1]), r, g, 3)
            if r == 0:
                ship(oa, 2)

        def products(g):
            for r in range(2):
                at = group_lanes(r, order[g - 1] % 4)
                x = own[:, at]
                wide = section == 0 and r == 0
                for m in range(3 if wide else 2) if section == 0 or r == 0 else (1,):
                    part[m] += dot(x, w[pl.ds(m * RANK, RANK), at], NT)
                if section == 0:
                    u = w[pl.ds(0, RANK), at]
                    gram[0] += dot(u, u, NT)
                    if wide:
                        gram[1] += dot(u, w[last, at], NT)
                    xf = x.astype(F32)
                    sq[...] += jnp.broadcast_to(jnp.sum(xf * xf, axis=1, keepdims=True), sq.shape)

        def far_products():
            for k in range(16):
                ref = w.at[got, pl.ds((16 + k) * BLK, BLK)]
                remote(ref, ref, ship_ss.at[0], ship_rs.at[k], diagonal).wait_recv()

            @pl.loop(0, 4)
            def _(k):
                at = pl.ds(pl.multiple_of((4 + k) * RING, RING), RING)
                part[2 if section == 0 else 0] += dot(own[:, at], w[got, at], NT)
                if section == 0:
                    gram[1] += dot(w[pl.ds(0, RANK), at], w[last, at], NT)

        local = both if section == 0 else pl.ds(RANK, 2 * RANK)
        for rows_now, sem in ((local, own_part_ss), (got, None)):
            if sem is None:
                ship(0, 0)
                pace()
                arrived(got, near, 0)
            for second in (False, True):
                for k, d in ((0, 1), (1, 3)):
                    go(spot(0, 0, 0, rows_now), 0, int(second), k, along(0, d, second),
                       None if sem is None else sem.at[int(second), k])
        arrived(kept, far, 2)
        first_sends(1)
        fill()
        part[...] = jnp.zeros_like(part)
        if section == 0:
            gram[...] = jnp.zeros_like(gram)
            sq[...] = jnp.zeros_like(sq)
        for r in range(2):
            for k, d in ((0, -1), (1, 1)):
                came(spot(r, d, 0), r, 0, k)
                go(spot(r, d, 0, halves[r][k]), r, 0, 2 + k, along(r, -d % 4, False))
                group_sends(r, 2 + k)
                if r == 0:
                    ship(d, 0)
        pace()
        for r in range(2):
            forward(r, 1)
        for r in range(2):
            came(spot(r, 2, 0, halves[r][0]), r, 0, 2)
            came(spot(r, 2, 0, halves[r][1]), r, 0, 3)
            group_sends(r, 4)
            if r == 0:
                ship(2, 0)
        pace()
        filled()
        for g in (2, 3, 4):
            for r in range(2):
                forward(r, g)
            pace()
            if g == 3:
                for r in range(2):
                    complete(r, 1)
                products(1)
        for g in (2, 3):
            for r in range(2):
                complete(r, g)
            products(g)
        for r in range(2):
            complete(r, 4)
        pace()
        products(4)

        def to_core(src, dst, k):
            copy = remote(src, dst, core_ss.at[k], core_rs.at[k], other_core)
            copy.start()
            return copy

        if section == 0:
            two, third = pl.ds(0, 2), pl.ds(2, 1)
            handed = [
                to_core(part.at[two, other_rows], got_part.at[two], 0),
                to_core(gram.at[0], got_gram.at[0], 1),
                to_core(sq.at[other_rows], got_sq, 2),
            ]
            far_products()
            handed.append(to_core(part.at[third, other_rows], got_part.at[third], 3))
            handed.append(to_core(gram.at[1], got_gram.at[1], 4))
            for copy in handed:
                copy.wait()
            pace()
        else:
            for m, k in ((1, 0), (0, 3)):
                if m == 0:
                    pace()
                    far_products()
                to_core(part.at[pl.ds(m, 1), other_rows], got_part.at[pl.ds(m, 1)], k).wait()
                sg[m] = (part[m, my_rows] + got_part[m]).astype(BF)
                from_later[m].start()
        return begun, started

    lr_mine, lr_other = lr.at[:, my_rows], lr.at[:, other_rows]
    bg_mine, bg_other = bg.at[:, my_rows], bg.at[:, other_rows]
    three = lr.at[pl.ds(0, 3), my_rows]
    three_other = lr.at[pl.ds(0, 3), other_rows]

    @pl.when(s == 1)
    def _():
        begun, started = gather(1)
        pl.loop(begun, 32)(exchange)
        for copy in from_later:
            copy.wait_send()
        remote(three, three, lr_ss.at[0], lr_rs.at[0], later).wait_recv()
        hand_on = remote(three, three, lr_ss.at[1], lr_rs.at[1], other_core)
        hand_on.start()
        remote(three_other, three_other, lr_ss.at[1], lr_rs.at[1], other_core).wait_recv()
        hand_on.wait_send()
        for copy in started:
            copy.wait_send()
        lrt[0] = lr[1].astype(F32).T.astype(BF)
        lrt[1] = lr[2].astype(F32).T.astype(BF)

    @pl.when(s == 0)
    def _():
        begun, started = gather(0)
        q0, p0, r = [part[m, my_rows] + got_part[m] for m in range(3)]
        uu = gram[0] + got_gram[0]
        ua = gram[1] + got_gram[1]
        sx = (sq[my_rows] + got_sq[...])[:, :1]
        inv0 = lax.rsqrt(sx * (1.0 / D) + EPSILON)
        pre0 = p0 * inv0
        sig0 = 1.0 / (1.0 + jnp.exp(-pre0))
        act0 = (pre0 * sig0).astype(BF)
        act0f = act0.astype(F32)
        t = dot_wide(act0, uu, NN)
        sb = sx + jnp.sum(act0f * (2.0 * q0 + t), axis=1, keepdims=True)
        inv1 = lax.rsqrt(jnp.maximum(sb, 0.0) * (1.0 / D) + EPSILON)
        p1 = r + dot_wide(act0, ua, NN)
        pre1 = p1 * inv1
        sig1 = 1.0 / (1.0 + jnp.exp(-pre1))
        act1 = (pre1 * sig1).astype(BF)
        from_later[1].wait_recv()
        pg1 = (got_sg[1].astype(F32) * sig1 * (1.0 + pre1 * (1.0 - sig1))).astype(BF).astype(F32)
        pg1s = (pg1 * inv1).astype(BF)
        lr[0, my_rows] = act0
        lr[1, my_rows] = pg1s
        lr[2, my_rows] = act1
        to_later = remote(three, three, lr_ss.at[0], lr_rs.at[0], later)
        to_later.start()
        pl.loop(begun, 32)(exchange)
        beta = inv1 * inv1 * inv1 * (jnp.sum(pg1 * p1, axis=1, keepdims=True) * (1.0 / D))
        from_later[0].wait_recv()
        ag0 = got_sg[0].astype(F32) + dot_wide(pg1s, ua, NT) - beta * (q0 + t)
        pg0 = (ag0 * sig0 * (1.0 + pre0 * (1.0 - sig0))).astype(BF).astype(F32)
        gamma = inv0 * inv0 * inv0 * (jnp.sum(pg0 * p0, axis=1, keepdims=True) * (1.0 / D))
        lr[3, my_rows] = (pg0 * inv0).astype(BF)
        bg[0, my_rows] = jnp.broadcast_to(beta, (ROWS, 128))
        bg[1, my_rows] = jnp.broadcast_to(gamma, (ROWS, 128))
        to_other = [
            remote(lr_mine, lr_mine, lr_ss.at[2], lr_rs.at[2], other_core),
            remote(bg_mine, bg_mine, lr_ss.at[3], lr_rs.at[3], other_core),
        ]
        for copy in to_other:
            copy.start()
        remote(lr_other, lr_other, lr_ss.at[2], lr_rs.at[2], other_core).wait_recv()
        remote(bg_other, bg_other, lr_ss.at[3], lr_rs.at[3], other_core).wait_recv()
        for copy in to_other + started:
            copy.wait_send()
        lrt[0] = lr[3].astype(F32).T.astype(BF)
        lrt[1] = lr[0].astype(F32).T.astype(BF)
        to_later.wait_send()

    top, bottom = pl.ds(0, RANK), pl.ds(RANK, RANK)

    def blocks(n, both=(1, 0), low=0, high=4):
        oa = FROM_BACK[n]

        @pl.loop(low, high)
        def _(j):
            ob = away(j)
            here = pl.ds(pl.multiple_of(ob * BLK, BLK), BLK)
            at = {r: lanes(r, oa, ob) for r in both}
            for r in both:
                new = oth.at[:, at[r]]
                remote(new, new, ex_ss, ex_rs.at[n * 4 + j, r], later).wait_recv()
                if oa in (1, 3):
                    k = oa // 2
                    src = r0.at[r, k, :, here]
                    remote(src, src, p0_ss, p0_rs.at[r, k, ob], later).wait_recv()

            def store(done, down, up):
                if oa == 1:
                    down = {r: down[r] + r0[r, 0, :, here].astype(F32) for r in both}
                if oa == 3:
                    up = {r: up[r] + r0[r, 1, :, here].astype(F32) for r in both}
                for r in both:
                    out[:, at[r]] = done[r]
                    gp[top, at[r]] = down[r].astype(BF)
                    gp[bottom, at[r]] = up[r].astype(BF)

            @pl.when(s == 0)
            def _():
                x, g = {r: own[:, at[r]] for r in both}, {r: oth[:, at[r]] for r in both}
                xf = {r: x[r].astype(F32) for r in both}
                beta = bg[0][:, :1]
                gamma = bg[1][:, :1]
                grown = {r: dot(lr[0], w[pl.ds(0, RANK), at[r]], NN) for r in both}
                slope = {r: dot(lr[1], w[pl.ds(2 * RANK, RANK), at[r]], NN) for r in both}
                bound = {r: (xf[r] + grown[r]).astype(BF).astype(F32) for r in both}
                passed = {r: (g[r].astype(F32) + slope[r] - beta * bound[r]).astype(BF) for r in both}
                first = {r: dot(lr[3], w[pl.ds(RANK, RANK), at[r]], NN) for r in both}
                down = {r: dot(lrt[0], x[r], NN) for r in both}
                up = {r: dot(lrt[1], passed[r], NN) for r in both}
                done = {r: (passed[r].astype(F32) + first[r] - gamma * xf[r]).astype(BF) for r in both}
                store(done, down, up)

            @pl.when(s == 1)
            def _():
                x, g = {r: oth[:, at[r]] for r in both}, {r: own[:, at[r]] for r in both}
                grown = {r: dot(lr[0], w[pl.ds(0, RANK), at[r]], NN) for r in both}
                final = {r: dot(lr[2], w[pl.ds(RANK, RANK), at[r]], NN) for r in both}
                up = {r: dot(lrt[1], g[r], NN) for r in both}
                bound = {r: (x[r].astype(F32) + grown[r]).astype(BF) for r in both}
                down = {r: dot(lrt[0], bound[r], NN) for r in both}
                done = {r: (bound[r].astype(F32) + final[r]).astype(BF) for r in both}
                store(done, down, up)

            for r in both:
                if oa == 2:
                    for k, rows, d in ((0, top, 1), (1, bottom, 3)):
                        remote(
                            gp.at[rows, at[r]], r0.at[r, k, :, here], p0_ss, p0_rs.at[r, k, ob],
                            along(r, d, False)).start()
                elif oa:
                    k = oa // 2
                    remote(
                        gp.at[:, at[r]], r1.at[r, k, :, here], p1_ss, p1_rs.at[r, k, ob], along(r, oa, False)).start()
            for r in both:
                there = res.at[:, feed_at(r, *place(r, oa, ob), c)]
                pltpu.make_async_copy(out.at[my_rows, at[r]], there, out_ls).start()
                remote(out.at[other_rows, at[r]], there, out_ss, out_rs, other_core).start()
            if oa == 0:
                for r in both:
                    total = gp[:, at[r]].astype(F32)
                    for k in range(2):
                        src = r1.at[r, k, :, here]
                        remote(src, src, p1_ss, p1_rs.at[r, k, ob], later).wait_recv()
                        total += src[...].astype(F32)

                    @pl.when(ob == 0)
                    def _():
                        tot[r] = total

                    @pl.when(ob != 0)
                    def _():
                        gp[:, at[r]] = total.astype(BF)
                        remote(
                            gp.at[:, at[r]], r2.at[r, ob - 1], p2_ss, p2_rs.at[r, ob - 1], along(r, ob, True)).start()

    def summed(r):
        total = tot[r]
        for k in range(3):
            remote(r2.at[r, k], r2.at[r, k], p2_ss, p2_rs.at[r, k], later).wait_recv()
            total += r2[r, k].astype(F32)
        return total

    for n in range(3):
        blocks(n)
    blocks(3, (1,))
    blocks(3, (0,), 0, 2)
    send3[...] = summed(1).astype(BF)
    across = remote(send3, r3, p3_ss, p3_rs, dev(dx=1))
    across.start()
    blocks(3, (0,), 2, 4)
    total = summed(0)
    across.wait()
    wg[...] = (total + r3[...].astype(F32)).T.astype(BF)

    there = own.at[other_rows, :]
    remote(there, there, own_ss, own_rs, other_core).wait_send()
    remote(oth, oth, ex_ss, ex_rs.at[0, 0], later).wait_send()
    ref = gp.at[top, pl.ds(0, 16 * BLK)]
    remote(ref, ref, p0_ss, p0_rs.at[0, 0, 0], later).wait_send()
    ref = gp.at[:, pl.ds(0, 16 * BLK)]
    remote(ref, ref, p1_ss, p1_rs.at[0, 0, 0], later).wait_send()
    ref = gp.at[:, pl.ds(0, 6 * BLK)]
    remote(ref, ref, p2_ss, p2_rs.at[0, 0], later).wait_send()
    half = out.at[my_rows, :]
    pltpu.make_async_copy(half, half, out_ls).wait()
    remote(half, half, out_ss, out_rs, other_core).wait()


def per_device(section_feeds, adapter_weights):
    shard = adapter_weights[0]
    feed = section_feeds[0].reshape(ROWS, D)
    dma = pltpu.SemaphoreType.DMA
    vm = pltpu.VMEM
    res, wg = pl.pallas_call(
        kernel,
        out_shape=(jax.ShapeDtypeStruct((ROWS, D), BF), jax.ShapeDtypeStruct((BLK, 2 * RANK), BF)),
        in_specs=[pl.BlockSpec(memory_space=pl.ANY), pl.BlockSpec(memory_space=pltpu.VMEM)],
        out_specs=(pl.BlockSpec(memory_space=pl.ANY), pl.BlockSpec(memory_space=pltpu.VMEM)),
        scratch_shapes=[
            vm((2 * ROWS, HALF), BF), vm((2 * ROWS, HALF), BF), vm((3 * RANK, HALF), BF),
            vm((2 * ROWS, HALF), BF), vm((2 * RANK, HALF), BF),
            vm((2, 2, RANK, RING), BF), vm((2, 2, 2 * RANK, RING), BF), vm((2, 3, 2 * RANK, BLK), BF),
            vm((2, 2 * RANK, BLK), F32), vm((2 * RANK, BLK), BF), vm((2 * RANK, BLK), BF),
            vm((3, 2 * ROWS, RANK), F32), vm((2, RANK, RANK), F32), vm((2 * ROWS, 128), F32),
            vm((3, ROWS, RANK), F32), vm((2, RANK, RANK), F32), vm((ROWS, 128), F32),
            vm((2, ROWS, RANK), BF), vm((2, ROWS, RANK), BF),
            vm((4, 2 * ROWS, RANK), BF), vm((2, 2 * ROWS, 128), F32), vm((2, RANK, 2 * ROWS), BF),
            dma, dma, dma, dma, dma((16, 2)), dma((3,)), dma((3,)),
            dma((2, 5, 4)), dma((2, 5, 4)), dma((2, 2)), dma((16,)), dma((16,)), dma((5,)), dma((5,)), dma((2,)), dma((2,)), dma((4,)), dma((4,)),
            dma, dma((2, 2, 4)), dma, dma((2, 2, 4)), dma, dma((2, 3)), dma, dma, dma, dma, dma,
        ],
        compiler_params=pltpu.CompilerParams(
            collective_id=0, has_side_effects=True, vmem_limit_bytes=44 * 2**20),
        cost_estimate=pl.CostEstimate(flops=8 * 10**9, bytes_accessed=10**7, transcendentals=0),
        name="relay",
    )(feed, shard)
    return res.reshape(section_feeds.shape), wg[None]


def solution(mesh):
    placed = (P("section", None, "fsdp", None), P("section", "fsdp", None))
    return jax.shard_map(per_device, mesh=mesh, in_specs=placed, out_specs=placed, check_vma=False)
```
